256 devices in a mesh: psg: 8 (over x, core), doc: 32 (over z, y).
Axes of the slice: x: 4, y: 4, z: 8, core: 2. Of those that a mesh axis runs over, the one named last changes fastest.
Arguments:
- hidden: bfloat16 [8, 32, 16, 128, 768], P(None, 'doc', 'psg'), may hold values from -6 to 6
- token_ids: int32 [8, 32, 16, 128], P(None, 'doc', 'psg'), may hold values from 0 to 30521, as said below
- passage_mask: int32 [8, 32, 16], P(None, 'doc', 'psg'), may hold values 0 or 1
- labels: int32 [8], replicated, may hold values from 0 to 31
- enc_weights: bfloat16 [4, 768, 768], replicated, may hold values from -0.21875 to 0.21875
- enc_gain: float32 [768], replicated, may hold values from 0.25 to 1.75
- agg_weights: bfloat16 [4, 768, 768], replicated, may hold values from -0.21875 to 0.21875
- agg_gain: float32 [768], replicated, may hold values from 0.25 to 1.75
- agg_cls: bfloat16 [768], replicated, may hold values from -6 to 6
- head_vector: float32 [768], replicated, may hold values from -1 to 1
- score_bias: float32 [], replicated, may hold values from 90 to 120
Outputs:
- scores: float32 [8, 32], P(None, 'doc')
- list_loss: float32 [], replicated
- weight_grads: float32 [2, 4, 589824], P(None, None, ('psg', 'doc'))
The draws below stay inside these ranges and needn't reach their ends.
Inputs may be any that keep to these rules, and one draw needn't show every extreme that they name: `token_ids`: each passage's ids are nonzero from its first position up to its length and zero after it; the first id is never zero.
All inputs are finite; a program needn't handle non-finite values. No bound on the sum of `passage_mask` on one device may be relied on, other than what follows from the above.
Results may differ from the reference program's by a relative error of at most 0.013.
Values may be sent and summed in bfloat16 or wider, within the bound.
No kernel may reach another device: no remote copies, remote signals or barrier semaphores. Data moves between devices by JAX's collectives and lax.ppermute only.
A program may use at most 128 MiB of HBM per device.

```python
import jax
import jax.numpy as jnp
from jax import lax

D = 768
HEADS = 12
HEAD = 64
VOCAB = 30522
SEQ = 128
QUERIES = 8
PSG = 16
CAND = 32


def draw_token_ids(key, part):
    key = jax.random.fold_in(key, 11)
    length_key, token_key = jax.random.split(key)
    lengths = jax.random.randint(length_key, (QUERIES, CAND, PSG, 1), SEQ // 4, SEQ + 1)
    token_vals = jax.random.randint(token_key, (QUERIES, CAND, PSG, SEQ), 1, VOCAB)
    position = jnp.arange(SEQ, dtype=jnp.int32)[None, None, None, :]
    return jnp.where(position < lengths, token_vals, 0).astype(jnp.int32)


def common_vector(key):
    return jnp.clip(jax.random.normal(key, (D,), jnp.float32), -4.0, 4.0)


def draw_head_vector(key, part):
    shared = common_vector(key)
    return (shared * D ** (-0.5)).astype(jnp.float32)


def draw_agg_cls(key, part):
    shared = common_vector(key)
    key = jax.random.fold_in(key, 22)
    noise = jnp.clip(jax.random.normal(key, (D,), jnp.float32), -4.0, 4.0)
    return (shared + 0.3 * noise).astype(jnp.bfloat16)


def set_ends(values, rng, smallest, high):
    place = [jax.random.randint(jax.random.fold_in(rng, axis), (), 0, length) for axis, length in enumerate(values.shape)]
    longest = values.shape.index(max(values.shape))
    neighbour = place[:longest] + [(place[longest] + 1) % values.shape[longest]] + place[longest + 1:]
    return values.at[tuple(place)].set(smallest).at[tuple(neighbour)].set(high)


def steps_of(key, dims, pieces, smallest, largest):
    loudness, own = 1.0, jax.random.fold_in(key, 6)
    for axis_at, blocks in pieces:
        steps = jnp.exp(jax.random.uniform(jax.random.fold_in(own, axis_at), (blocks,), jnp.float32, smallest / len(pieces), largest / len(pieces)))
        loudness = loudness * jnp.repeat(steps, dims[axis_at] // blocks).reshape([-1 if axis == axis_at else 1 for axis in range(len(dims))])
    return loudness


def normal_values(rng, extent, width, bound, shards=(), kind=jnp.bfloat16):
    entries = width * jax.random.normal(rng, extent, jnp.float32)
    if shards:
        entries = entries * steps_of(rng, extent, shards, -0.22, 0.18)
    return jnp.clip(entries, -bound, bound).astype(kind)


def setup_inputs(seed: int = 0) -> dict:
    streams_of = jax.random.split(jax.random.key(seed), 12)
    hidden = normal_values(streams_of[0], (QUERIES, CAND, PSG, SEQ, D), 1.0, 6.0, ((1, 32), (2, 8)))
    token_ids = draw_token_ids(jax.random.fold_in(streams_of[11], 71), 0)
    passage_mask = set_ends((jax.random.randint(streams_of[2], (QUERIES, CAND, PSG), 0, 4) < 3).astype(jnp.int32), jax.random.fold_in(streams_of[2], 1), 0, 1)
    labels = set_ends(jax.random.randint(streams_of[3], (QUERIES,), 0, CAND), jax.random.fold_in(streams_of[3], 1), 0, CAND - 1).astype(jnp.int32)
    enc_weights = normal_values(streams_of[4], (4, D, D), D ** -0.5, 0.21875)
    enc_gain = jnp.clip(1.0 + 0.15 * jax.random.normal(streams_of[5], (D,), jnp.float32), 0.25, 1.75)
    agg_weights = normal_values(streams_of[6], (4, D, D), D ** -0.5, 0.21875)
    agg_gain = jnp.clip(1.0 + 0.15 * jax.random.normal(streams_of[7], (D,), jnp.float32), 0.25, 1.75)
    agg_cls = draw_agg_cls(jax.random.fold_in(streams_of[11], 71), 0)
    head_vector = draw_head_vector(jax.random.fold_in(streams_of[11], 71), 0)
    score_bias = jnp.clip(jax.random.uniform(streams_of[10], (), jnp.float32, 90.0, 120.0), 90.0, 120.0)
    return dict(hidden=hidden, token_ids=token_ids, passage_mask=passage_mask, labels=labels, enc_weights=enc_weights, enc_gain=enc_gain, agg_weights=agg_weights, agg_gain=agg_gain, agg_cls=agg_cls, head_vector=head_vector, score_bias=score_bias)


exact_mode = lax.Precision.HIGHEST

def inner_rows(left, right):
    return lax.dot_general(left, right, (((0,), (0,)), ((), ())), preferred_element_type=jnp.float32)

def outer_rows(left, weight):
    return lax.dot_general(left, weight, (((1,), (1,)), ((), ())), preferred_element_type=jnp.float32)

def layer_norm(inputs, norm_gain):
    center = inputs - lax.optimization_barrier(jnp.mean(inputs, axis=-1, keepdims=True))
    rscale = lax.rsqrt(lax.optimization_barrier(jnp.mean(center * center, axis=-1, keepdims=True)) + 1e-05)
    normed = center * rscale
    return (normed * norm_gain, normed, rscale)

def norm_back(grad_out, norm_gain, normed, rscale):
    grad_norm = grad_out * norm_gain
    return rscale * (grad_norm - lax.optimization_barrier(jnp.mean(grad_norm, axis=-1, keepdims=True)) - normed * lax.optimization_barrier(jnp.mean(grad_norm * normed, axis=-1, keepdims=True)))

def encode(states, id_rows, enc_weights, enc_gain):
    row_count, length, model_width = states.shape
    flat_rows = states.reshape(row_count * length, model_width)
    pass_keys = jnp.dot(flat_rows, enc_weights[1], preferred_element_type=jnp.float32).reshape(row_count, length, HEADS, HEAD)
    values = jnp.dot(flat_rows, enc_weights[2], preferred_element_type=jnp.float32).reshape(row_count, length, HEADS, HEAD)
    first_rows = states[:, 0, :]
    cls_query = jnp.dot(first_rows, enc_weights[0], preferred_element_type=jnp.float32).reshape(row_count, HEADS, HEAD)
    valid_keys = (id_rows != 0)[:, None, :]
    logits = jnp.einsum('phe,pshe->phs', cls_query, pass_keys, precision=exact_mode) * HEAD ** (-0.5)
    logits = jnp.where(valid_keys, logits, -1e+30)
    peak_val = lax.optimization_barrier(jnp.max(logits, axis=-1, keepdims=True))
    raw_weights = jnp.where(valid_keys, jnp.exp(logits - peak_val), 0.0)
    soft_weights = raw_weights / lax.optimization_barrier(jnp.sum(raw_weights, axis=-1, keepdims=True))
    attended = jnp.einsum('phs,pshe->phe', soft_weights, values, precision=exact_mode)
    attended_b = attended.reshape(row_count, model_width).astype(jnp.bfloat16)
    mixed_rows = first_rows.astype(jnp.float32) + jnp.dot(attended_b, enc_weights[3], preferred_element_type=jnp.float32)
    passage, normed, rscale = layer_norm(mixed_rows, enc_gain)
    saved = (pass_keys, values, cls_query, soft_weights, attended, attended_b, normed, rscale)
    return (passage.astype(jnp.bfloat16), saved)

def encode_back(states, saved, grad_passage, enc_weights, enc_gain):
    pass_keys, values, cls_query, soft_weights, attended, attended_b, normed, rscale = saved
    row_count, length, model_width = states.shape
    grad_mixed = norm_back(grad_passage, enc_gain, normed, rscale).astype(jnp.bfloat16)
    grad_out_w = inner_rows(attended_b, grad_mixed)
    grad_att = outer_rows(grad_mixed, enc_weights[3]).reshape(row_count, HEADS, HEAD)
    grad_values = jnp.einsum('phs,phe->pshe', soft_weights, grad_att, precision=exact_mode)
    along_val = jnp.einsum('phe,pshe->phs', grad_att, values, precision=exact_mode)
    base_dot = lax.optimization_barrier(jnp.sum(grad_att * attended, axis=-1, keepdims=True))
    grad_logits = soft_weights * (along_val - base_dot) * HEAD ** (-0.5)
    grad_keys = jnp.einsum('phs,phe->pshe', grad_logits, cls_query, precision=exact_mode)
    grad_query = jnp.einsum('phs,pshe->phe', grad_logits, pass_keys, precision=exact_mode).reshape(row_count, model_width)
    flat_rows = states.reshape(row_count * length, model_width)
    grad_key_w = inner_rows(flat_rows, grad_keys.reshape(row_count * length, model_width).astype(jnp.bfloat16))
    grad_value_w = inner_rows(flat_rows, grad_values.reshape(row_count * length, model_width).astype(jnp.bfloat16))
    grad_query_w = inner_rows(states[:, 0, :], grad_query.astype(jnp.bfloat16))
    return jnp.stack([grad_query_w, grad_key_w, grad_value_w, grad_out_w])

def pool_local(flat_pass, mask_rows, agg_weights, agg_cls):
    doc_count, slot_count = mask_rows.shape
    cls_row = agg_cls[None, :]
    cls_query = jnp.dot(cls_row, agg_weights[0], preferred_element_type=jnp.float32).reshape(HEADS, HEAD)
    cls_key = jnp.dot(cls_row, agg_weights[1], preferred_element_type=jnp.float32).reshape(HEADS, HEAD)
    cls_value = jnp.dot(cls_row, agg_weights[2], preferred_element_type=jnp.float32).reshape(HEADS, HEAD)
    pass_keys = jnp.dot(flat_pass, agg_weights[1], preferred_element_type=jnp.float32).reshape(doc_count, slot_count, HEADS, HEAD)
    values = jnp.dot(flat_pass, agg_weights[2], preferred_element_type=jnp.float32).reshape(doc_count, slot_count, HEADS, HEAD)
    valid_keys = (mask_rows != 0)[:, None, :]
    logits = jnp.einsum('he,pshe->phs', cls_query, pass_keys, precision=exact_mode) * HEAD ** (-0.5)
    logits = jnp.where(valid_keys, logits, -1e+30)
    peak_local = lax.optimization_barrier(jnp.max(logits, axis=-1))
    raw_weights = jnp.where(valid_keys, jnp.exp(logits - peak_local[..., None]), 0.0)
    total_local = lax.optimization_barrier(jnp.sum(raw_weights, axis=-1))
    sums_local = jnp.einsum('phs,pshe->phe', raw_weights, values, precision=exact_mode).reshape(doc_count, HEADS * HEAD)
    extras = (cls_query, cls_key, cls_value, pass_keys, values, logits, valid_keys)
    return ((peak_local, total_local, sums_local), extras)

def pool_finish(merged, extras, agg_weights, agg_gain, agg_cls, head_vector, score_bias):
    peak_m, total_m, sums_m = merged
    cls_query, cls_key, cls_value, pass_keys, values, logits, valid_keys = extras
    doc_count = peak_m.shape[0]
    cls_logit = lax.optimization_barrier(jnp.sum(cls_query * cls_key, axis=-1)) * HEAD ** (-0.5)
    peak_val = jnp.maximum(peak_m, cls_logit[None, :])
    factor = jnp.exp(peak_m - peak_val)
    cls_raw = jnp.exp(cls_logit[None, :] - peak_val)
    totals = total_m * factor + cls_raw
    pooled = (sums_m.reshape(doc_count, HEADS, HEAD) * factor[..., None] + cls_raw[..., None] * cls_value[None]) / totals[..., None]
    soft_weights = jnp.where(valid_keys, jnp.exp(logits - peak_val[..., None]), 0.0) / totals[..., None]
    cls_prob = cls_raw / totals
    pooled_b = pooled.reshape(doc_count, HEADS * HEAD).astype(jnp.bfloat16)
    mixed_rows = agg_cls.astype(jnp.float32)[None, :] + jnp.dot(pooled_b, agg_weights[3], preferred_element_type=jnp.float32)
    normal_out, normed, rscale = layer_norm(mixed_rows, agg_gain)
    score_rows = score_bias + lax.optimization_barrier(jnp.sum(normal_out * head_vector[None, :], axis=-1))
    saved = (cls_query, cls_key, cls_value, pass_keys, values, soft_weights, cls_prob, pooled, pooled_b, normed, rscale)
    return (score_rows, saved)

def pool_back(grad_score, saved, flat_pass, agg_weights, agg_gain, agg_cls, head_vector, lead_flag):
    cls_query, cls_key, cls_value, pass_keys, values, soft_weights, cls_prob, pooled, pooled_b, normed, rscale = saved
    doc_count, slot_count = (soft_weights.shape[0], soft_weights.shape[2])
    model_width = flat_pass.shape[1]
    scale_qk = HEAD ** (-0.5)
    grad_out = grad_score[:, None] * head_vector[None, :]
    grad_mixed = norm_back(grad_out, agg_gain, normed, rscale).astype(jnp.bfloat16)
    grad_out_w = inner_rows(pooled_b, grad_mixed) * lead_flag
    grad_pool = outer_rows(grad_mixed, agg_weights[3]).reshape(doc_count, HEADS, HEAD)
    base_dot = lax.optimization_barrier(jnp.sum(grad_pool * pooled, axis=-1))
    grad_values = jnp.einsum('phs,phe->pshe', soft_weights, grad_pool, precision=exact_mode)
    along_val = jnp.einsum('phe,pshe->phs', grad_pool, values, precision=exact_mode)
    grad_logits = soft_weights * (along_val - base_dot[..., None]) * scale_qk
    grad_keys = jnp.einsum('phs,he->pshe', grad_logits, cls_query, precision=exact_mode)
    cls_grad_value = cls_prob[..., None] * grad_pool
    cls_grad_logit = cls_prob * (lax.optimization_barrier(jnp.sum(grad_pool * cls_value[None], axis=-1)) - base_dot) * scale_qk
    cls_grad_key = cls_grad_logit[..., None] * cls_query[None]
    grad_query = jnp.einsum('phs,pshe->he', grad_logits, pass_keys, precision=exact_mode) + lead_flag * jnp.einsum('ph,he->he', cls_grad_logit, cls_key, precision=exact_mode)
    cls_float = agg_cls.astype(jnp.float32)
    key_rows = grad_keys.reshape(doc_count * slot_count, model_width).astype(jnp.bfloat16)
    value_rows = grad_values.reshape(doc_count * slot_count, model_width).astype(jnp.bfloat16)
    grad_query_w = cls_float[:, None] * grad_query.reshape(model_width)[None, :]
    grad_key_w = inner_rows(flat_pass, key_rows) + lead_flag * cls_float[:, None] * lax.optimization_barrier(jnp.sum(cls_grad_key, axis=0)).reshape(model_width)[None, :]
    grad_value_w = inner_rows(flat_pass, value_rows) + lead_flag * cls_float[:, None] * lax.optimization_barrier(jnp.sum(cls_grad_value, axis=0)).reshape(model_width)[None, :]
    grad_pass = outer_rows(key_rows, agg_weights[1]) + outer_rows(value_rows, agg_weights[2])
    return (jnp.stack([grad_query_w, grad_key_w, grad_value_w, grad_out_w]), grad_pass)

def reference(hidden, token_ids, passage_mask, labels, enc_weights, enc_gain, agg_weights, agg_gain, agg_cls, head_vector, score_bias):
    doc_count = QUERIES * CAND
    block_states = hidden.reshape(doc_count, PSG, SEQ, D)
    block_ids = token_ids.reshape(doc_count, PSG, SEQ)

    def forward_block(current):
        return encode(current[0], current[1], enc_weights, enc_gain)[0]
    passages = lax.map(forward_block, (block_states, block_ids))
    flat_pass = passages.reshape(doc_count * PSG, D)
    local_stats, extras = pool_local(flat_pass, passage_mask.reshape(doc_count, PSG), agg_weights, agg_cls)
    score_rows, saved = pool_finish(local_stats, extras, agg_weights, agg_gain, agg_cls, head_vector, score_bias)
    scores = score_rows.reshape(QUERIES, CAND)
    peak_val = lax.optimization_barrier(jnp.max(scores, axis=1))
    totals = lax.optimization_barrier(jnp.sum(jnp.exp(scores - peak_val[:, None]), axis=1))
    label_hits = (labels[:, None] == jnp.arange(CAND, dtype=jnp.int32)[None, :]).astype(jnp.float32)
    label_score = lax.optimization_barrier(jnp.sum(scores * label_hits, axis=1))
    list_loss = jnp.mean(jnp.log(totals) + peak_val - label_score)
    grad_score = (jnp.exp(scores - peak_val[:, None]) / totals[:, None] - label_hits) / QUERIES
    agg_grads, grad_pass = pool_back(grad_score.reshape(doc_count), saved, flat_pass, agg_weights, agg_gain, agg_cls, head_vector, 1.0)
    grad_blocks = grad_pass.reshape(doc_count, PSG, D)

    def backward_block(running, current):
        states, id_rows, grad_rows = current
        passage, enc_saved = encode(states, id_rows, enc_weights, enc_gain)
        return (running + encode_back(states, enc_saved, grad_rows, enc_weights, enc_gain), None)
    enc_grads, _ = lax.scan(backward_block, jnp.zeros((4, D, D), jnp.float32), (block_states, block_ids, grad_blocks))
    weight_grads = jnp.stack([enc_grads, agg_grads]).reshape(2, 4, D * D)
    return (scores, list_loss, weight_grads)
```

```python
import jax
import jax.numpy as jnp
from jax import lax
from jax.experimental import pallas as pl
from jax.experimental.pallas import tpu as pltpu
from jax.sharding import PartitionSpec as P

HEADS = 12
HEAD = 64
D = 768
SEQ = 128
QUERIES = 8
SLOTS = 2
LOCAL = QUERIES * SLOTS
PSG_DEV = 8
DOC_DEV = 32
GROUP = PSG_DEV * LOCAL
ROWS = D // PSG_DEV
SHARE = ROWS // DOC_DEV
PAD_HEADS = 16
PAY = 120
SCALE = HEAD ** (-0.5)
VMEM_LIMIT = 56 * 1024 * 1024

f32 = jnp.float32
bf16 = jnp.bfloat16


def dot_nn(a, b):
    return lax.dot_general(a, b, (((1,), (0,)), ((), ())), preferred_element_type=f32)


def dot_nt(a, b):
    return lax.dot_general(a, b, (((1,), (1,)), ((), ())), preferred_element_type=f32)


def dot_tn(a, b):
    return lax.dot_general(a, b, (((0,), (0,)), ((), ())), preferred_element_type=f32)


def halves(x):
    hi = x.astype(bf16)
    lo = (x - hi.astype(f32)).astype(bf16)
    return hi, lo


def two_part(dot, x, w):
    n = x.shape[0]
    both = dot(jnp.concatenate(halves(x), axis=0), w)
    return both[:n] + both[n:]


def iota(shape, dim):
    return lax.broadcasted_iota(jnp.int32, shape, dim)


def head_mask():
    return iota((PAD_HEADS, D), 0) == (iota((PAD_HEADS, D), 1) >> 6)


def spread(rows, mask):
    n = rows.shape[0]
    wide = jnp.where(mask[None], rows[:, None, :], 0.0)
    return wide.reshape(n * PAD_HEADS, D)


def fold(rows, mask):
    n = rows.shape[0] // PAD_HEADS
    wide = jnp.where(mask[None], rows.reshape(n, PAD_HEADS, D), 0.0)
    return jnp.sum(wide, axis=1)


def norm_parts(x):
    center = x - jnp.mean(x, axis=-1, keepdims=True)
    rscale = lax.rsqrt(jnp.mean(center * center, axis=-1, keepdims=True) + 1e-05)
    return center * rscale, rscale


def norm_back(grad_out, gain, normed, rscale):
    grad_norm = grad_out * gain
    return rscale * (
        grad_norm
        - jnp.mean(grad_norm, axis=-1, keepdims=True)
        - normed * jnp.mean(grad_norm * normed, axis=-1, keepdims=True)
    )


def pick_rows(first):
    r = iota((ROWS, D), 0)
    want = first + SHARE * (r & (DOC_DEV - 1)) + (r >> 5)
    return jnp.where(iota((ROWS, D), 1) == want, 1.0, 0.0).astype(bf16)


def forward_kernel(
    hid_ref, ids_ref, mask_ref, far_ref, pay_ref, soft_ref, z_ref, h0_s, z_s, we_ref, sems
):
    loads = [pltpu.make_async_copy(far_ref.at[n], we_ref.at[n], sems.at[n]) for n in range(3)]
    for load in loads:
        load.start()
    order = [(q, sl) for sl in range(SLOTS) for q in range(QUERIES)]
    for p, (q, sl) in enumerate(order):
        h0_s[p : p + 1, :] = hid_ref[q, sl, 0:16, :].astype(f32)[0:1, :]
    mask = head_mask()
    h0 = h0_s[...].astype(bf16)
    loads[0].wait()
    query = dot_nn(h0, we_ref[0]) * SCALE
    loads[1].wait()
    qk = two_part(dot_nt, spread(query, mask), we_ref[1])
    qk_hi, qk_lo = halves(qk)
    logits, valid = [], []
    for p, (q, sl) in enumerate(order):
        at = slice(p * PAD_HEADS, (p + 1) * PAD_HEADS)
        both = dot_nt(jnp.concatenate([qk_hi[at], qk_lo[at]], axis=0), hid_ref[q, sl])
        logits.append(both[:PAD_HEADS] + both[PAD_HEADS:])
        valid.append(jnp.broadcast_to(ids_ref[q, sl : sl + 1, :], (PAD_HEADS, SEQ)))
    logits = jnp.concatenate(logits, axis=0)
    valid = jnp.concatenate(valid, axis=0) != 0
    logits = jnp.where(valid, logits, -1e30)
    peak = jnp.max(logits, axis=-1, keepdims=True)
    raw = jnp.where(valid, jnp.exp(logits - peak), 0.0)
    soft = raw / jnp.sum(raw, axis=-1, keepdims=True)
    soft_ref[...] = soft
    soft_hi, soft_lo = halves(soft)
    z_all = []
    for p, (q, sl) in enumerate(order):
        at = slice(p * PAD_HEADS, (p + 1) * PAD_HEADS)
        both = dot_nn(jnp.concatenate([soft_hi[at], soft_lo[at]], axis=0), hid_ref[q, sl])
        z = both[:PAD_HEADS] + both[PAD_HEADS:]
        z_all.append(z)
        for c in range(D // 128):
            z_s[c, pl.ds(p, PAD_HEADS, stride=LOCAL), :] = z[:, c * 128 : (c + 1) * 128]
    z_all = jnp.concatenate(z_all, axis=0)
    for c in range(D // 128):
        z_ref[:, c * 128 : (c + 1) * 128] = z_s[c, : HEADS * LOCAL, :].astype(bf16)
    loads[2].wait()
    attended = fold(two_part(dot_nn, z_all, we_ref[2]), mask).astype(bf16)
    keep = mask_ref[...]
    keep = jnp.concatenate(
        [jnp.broadcast_to(keep[:, sl : sl + 1], (QUERIES, 128)) for sl in range(SLOTS)], axis=0
    )
    keep = jnp.where(keep != 0, 1.0, 0.0).astype(bf16)
    row = jnp.concatenate([h0, attended, keep], axis=1)
    for i in range(PSG_DEV):
        pay_ref[i] = row


def backward_kernel(
    got_ref,
    hid_ref,
    soft_ref,
    z_ref,
    we_ref,
    gain_e_ref,
    wa_ref,
    gain_a_ref,
    cls_ref,
    head_ref,
    bias_ref,
    score_ref,
    pay_ref,
    query_ref,
    gatt_ref,
    gmix_ref,
    zagg_ref,
    pooled_ref,
    small_ref,
    m_ref,
    u_s,
):
    me = lax.axis_index("psg")
    mask = head_mask()
    got = got_ref[...].reshape(GROUP, 2 * D + 128)
    h0 = got[:, :D]
    att = got[:, D : 2 * D]
    keep = got[:, 2 * D :]
    query_ref[...] = dot_nn(h0, we_ref[0])
    gain_e = gain_e_ref[...]
    gain_a = gain_a_ref[...]
    head = head_ref[...]
    cls_b = cls_ref[...]
    cls_f = cls_b.astype(f32)
    normed_e, rscale_e = norm_parts(h0.astype(f32) + dot_nn(att, we_ref[3]))
    passage = (normed_e * gain_e).astype(bf16)

    cls_8 = jnp.broadcast_to(cls_f, (QUERIES, D)).astype(bf16)
    cls_query = dot_nn(cls_8, wa_ref[0])
    kq = two_part(dot_nt, jnp.where(mask, cls_query[0:1], 0.0), wa_ref[1])
    logit = two_part(dot_nt, kq, passage) * SCALE
    cls_logit = jnp.sum(kq * cls_f, axis=-1, keepdims=True) * SCALE
    lane_one = jnp.where(iota((16, 128), 1) == 0, 1.0, 0.0).astype(bf16)
    present = dot_nt(lane_one, keep)
    shape3 = (QUERIES, PAD_HEADS, GROUP)
    valid = ((iota(shape3, 2) & (QUERIES - 1)) == iota(shape3, 0)) & (present[None] > 0.5)
    logit3 = jnp.where(valid, logit[None], -1e30)
    peak = jnp.maximum(jnp.max(logit3, axis=-1, keepdims=True), cls_logit[None])
    raw = jnp.where(valid, jnp.exp(logit3 - peak), 0.0)
    cls_raw = jnp.exp(cls_logit[None] - peak)
    total = jnp.sum(raw, axis=-1, keepdims=True) + cls_raw
    soft = (raw / total).reshape(QUERIES * PAD_HEADS, GROUP)
    cls_prob = (cls_raw / total).reshape(QUERIES * PAD_HEADS, 1)
    zagg = two_part(dot_nn, soft, passage) + cls_prob * cls_f
    zagg_ref[...] = zagg.astype(bf16)
    pooled = fold(two_part(dot_nn, zagg, wa_ref[2]), mask)
    pooled_b = jnp.concatenate([pooled, jnp.zeros_like(pooled)], axis=0).astype(bf16)
    pooled_ref[...] = pooled_b
    mixed_a = cls_f + dot_nn(pooled_b, wa_ref[3])[:QUERIES]
    normed_a, rscale_a = norm_parts(mixed_a)
    score = bias_ref[0, 0] + jnp.sum(normed_a * gain_a * head, axis=-1, keepdims=True)
    score = jnp.broadcast_to(score, (QUERIES, 128))
    for j in range(DOC_DEV):
        score_ref[j] = score

    gmix_a = norm_back(jnp.broadcast_to(head, (QUERIES, D)), gain_a, normed_a, rscale_a)
    gmix_a16 = jnp.concatenate([gmix_a, jnp.zeros_like(gmix_a)], axis=0).astype(bf16)
    gpool = dot_nt(gmix_a16, wa_ref[3])[:QUERIES]
    gpv = two_part(dot_nt, spread(gpool, mask), wa_ref[2])
    base = jnp.sum(gpv * zagg, axis=-1, keepdims=True)
    along = two_part(dot_nt, gpv, passage)
    glogit = soft * (along - base) * SCALE
    cls_glogit = cls_prob * (jnp.sum(gpv * cls_f, axis=-1, keepdims=True) - base) * SCALE
    m = two_part(dot_nn, glogit, passage) + cls_glogit * cls_f
    m_ref[...] = m
    small_ref[0] = gpool
    small_ref[1] = gmix_a
    small_ref[2] = fold(two_part(dot_nn, m, wa_ref[1]), mask)
    small_ref[3] = cls_query
    kq_wide = jnp.broadcast_to(kq[None], (QUERIES, PAD_HEADS, D)).reshape(QUERIES * PAD_HEADS, D)
    left = jnp.concatenate([glogit, soft], axis=0).astype(bf16)
    right = jnp.concatenate([kq_wide, gpv], axis=0).astype(bf16)
    gpass = dot_tn(left, right)

    gmix_e = norm_back(gpass, gain_e, normed_e, rscale_e)
    gmix_ref[...] = gmix_e
    gatt_ref[...] = dot_nt(gmix_e.astype(bf16), we_ref[3])
    mine = gatt_ref[pl.ds(pl.multiple_of(me * LOCAL, LOCAL), LOCAL), :]
    wv = two_part(dot_nt, spread(mine, mask), we_ref[2])
    wv_hi, wv_lo = halves(wv)
    order = [(q, sl) for sl in range(SLOTS) for q in range(QUERIES)]
    along_e = []
    for p, (q, sl) in enumerate(order):
        at = slice(p * PAD_HEADS, (p + 1) * PAD_HEADS)
        both = dot_nt(jnp.concatenate([wv_hi[at], wv_lo[at]], axis=0), hid_ref[q, sl])
        along_e.append(both[:PAD_HEADS] + both[PAD_HEADS:])
    along_e = jnp.concatenate(along_e, axis=0)
    soft_e = soft_ref[...]
    base_e = jnp.sum(soft_e * along_e, axis=-1, keepdims=True)
    gl_hi, gl_lo = halves(soft_e * (along_e - base_e) * SCALE)
    u_all = []
    for p, (q, sl) in enumerate(order):
        at = slice(p * PAD_HEADS, (p + 1) * PAD_HEADS)
        both = dot_nn(jnp.concatenate([gl_hi[at], gl_lo[at]], axis=0), hid_ref[q, sl])
        u = both[:PAD_HEADS] + both[PAD_HEADS:]
        u_all.append(u)
        for c in range(D // 128):
            u_s[c, pl.ds(p, PAD_HEADS, stride=LOCAL), :] = u[:, c * 128 : (c + 1) * 128]
    u_all = jnp.concatenate(u_all, axis=0)
    gquery = fold(two_part(dot_nn, u_all, we_ref[1]), mask).astype(bf16)
    u_rows = jnp.concatenate([u_s[c, : HEADS * LOCAL, :] for c in range(D // 128)], axis=1).astype(bf16)
    zu = jnp.concatenate([z_ref[...], u_rows[128:], u_rows[:128]], axis=0)
    for i in range(PSG_DEV):
        pay_ref[i, :ROWS, :] = dot_nt(pick_rows(ROWS * i), zu).astype(bf16)
        pay_ref[i, ROWS : ROWS + 16, :] = gquery[:, : D // 2]
        pay_ref[i, ROWS + 16 :, :] = gquery[:, D // 2 :]


def weights_kernel(
    all_ref,
    own_ref,
    labels_ref,
    recv_ref,
    got_ref,
    query_ref,
    gatt_ref,
    gmix_ref,
    zagg_ref,
    pooled_ref,
    small_ref,
    m_ref,
    pay_ref,
    loss_ref,
    out_s,
):
    me = lax.axis_index("psg")
    doc = lax.axis_index("doc")
    everything = all_ref[...]
    labels = jnp.broadcast_to(labels_ref[...], (QUERIES, 128))
    peak = jnp.max(everything, axis=0)
    total = jnp.sum(jnp.exp(everything - peak[None]), axis=0)
    hits = iota((DOC_DEV, QUERIES, 128), 0) == labels[None]
    label_score = jnp.sum(jnp.where(hits, everything, 0.0), axis=0)
    losses = jnp.log(total) + peak - label_score
    loss_ref[...] = jnp.sum(losses[:, 0:1], axis=0, keepdims=True) / QUERIES
    own_hit = jnp.where(labels == doc, 1.0, 0.0)
    g8 = (jnp.exp(own_ref[0] - peak) / total - own_hit) / QUERIES
    g8 = jnp.broadcast_to(g8[:, 0:1], (QUERIES, D))
    g16 = jnp.concatenate([g8, g8], axis=0)
    g_group = jnp.concatenate([g16] * PSG_DEV, axis=0)
    g_heads = jnp.broadcast_to(g8[:, None, :], (QUERIES, PAD_HEADS, D)).reshape(QUERIES * PAD_HEADS, D)
    mask = head_mask()

    def put(at, rows):
        for k in range(SHARE):
            for c in range(D // 128):
                out_s[pl.ds(at + k * (D // 128) + c, DOC_DEV, stride=PAY), :] = rows[
                    k * DOC_DEV : (k + 1) * DOC_DEV, c * 128 : (c + 1) * 128
                ]

    pick = pick_rows(me * ROWS)
    got = got_ref[...].reshape(GROUP, 2 * D + 128)
    gq = jnp.concatenate(
        [
            jnp.concatenate([recv_ref[s, ROWS : ROWS + 16, :], recv_ref[s, ROWS + 16 :, :]], axis=1)
            for s in range(PSG_DEV)
        ],
        axis=0,
    )
    h0_t = dot_nt(pick, got[:, :D]).astype(bf16)
    put(0, dot_nn(h0_t, (gq.astype(f32) * g_group).astype(bf16)))
    att_t = dot_nt(pick, got[:, D : 2 * D]).astype(bf16)
    put(54, dot_nn(att_t, (gmix_ref[...] * g_group).astype(bf16)))
    key_head = iota((16, D), 0)
    key_head = jnp.where(key_head < 4, -1, jnp.where(key_head < 8, key_head + 4, key_head - 8))
    key_mask = key_head == (iota((16, D), 1) >> 6)
    gk = jnp.zeros((ROWS, D), f32)
    gv = jnp.zeros((ROWS, D), f32)
    for s in range(PSG_DEV):
        at = slice(s * LOCAL, (s + 1) * LOCAL)
        q_rows = query_ref[at, :] * g16
        a_rows = gatt_ref[at, :] * g16
        q_wide = jnp.where(key_mask[:, None, :], q_rows[None], 0.0).reshape(16 * LOCAL, D)
        a_wide = jnp.where(mask[:, None, :], a_rows[None], 0.0).reshape(16 * LOCAL, D)
        gv = gv + dot_nn(recv_ref[s, :ROWS, :256], a_wide.astype(bf16))
        gk = gk + dot_nn(recv_ref[s, :ROWS, 128:], q_wide.astype(bf16))
    put(18, gk)
    put(36, gv)
    za_t = dot_nt(pick, zagg_ref[...]).astype(bf16)
    put(72, dot_nn(za_t, spread(small_ref[0] * g8, mask).astype(bf16)))
    pooled_t = dot_nt(pick, pooled_ref[...]).astype(bf16)
    gmix_a = small_ref[1] * g8
    gmix_a = jnp.concatenate([gmix_a, jnp.zeros_like(gmix_a)], axis=0).astype(bf16)
    put(90, dot_nn(pooled_t, gmix_a))
    qvec = jnp.sum(small_ref[2] * g8, axis=0, keepdims=True)
    for c in range(D // 128):
        out_s[pl.ds(108 + c, DOC_DEV, stride=PAY), :] = jnp.broadcast_to(
            qvec[:, c * 128 : (c + 1) * 128], (DOC_DEV, 128)
        )
    m_sum = jnp.sum((m_ref[...] * g_heads).reshape(QUERIES, PAD_HEADS, D), axis=0)
    m_tile = jnp.concatenate([m_sum] * 8, axis=0)
    m_hi, m_lo = halves(m_tile)
    m_t = dot_nt(pick, m_hi) + dot_nt(pick, m_lo)
    lane_k = iota((DOC_DEV, 128), 1) >> 4
    m_row = jnp.zeros((DOC_DEV, 128), f32)
    for k in range(SHARE):
        m_row = jnp.where(lane_k == k, m_t[k * DOC_DEV : (k + 1) * DOC_DEV], m_row)
    out_s[pl.ds(114, DOC_DEV, stride=PAY), :] = m_row
    for r in range(115, PAY):
        out_s[pl.ds(r, DOC_DEV, stride=PAY), :] = jnp.zeros((DOC_DEV, 128), f32)
    pay_ref[...] = out_s[...].astype(bf16).reshape(DOC_DEV, PAY, 128)


def finish_kernel(recv_ref, small_ref, cls_ref, out_ref):
    first = lax.axis_index("psg") * ROWS + lax.axis_index("doc") * SHARE
    total = recv_ref[0].astype(f32)
    for j in range(1, DOC_DEV):
        total = total + recv_ref[j].astype(f32)
    place = {0: (0, 0), 18: (0, 1), 36: (0, 2), 54: (0, 3), 72: (1, 2), 90: (1, 3)}
    for at, (layer, proj) in place.items():
        for r in range(18):
            out_ref[layer, proj : proj + 1, r * 128 : (r + 1) * 128] = total[at + r : at + r + 1, :]
    cls_f = cls_ref[...].astype(f32)
    m_row = jnp.broadcast_to(total[114:115, :], (16, 128))
    m_row = jnp.where((iota((16, 128), 1) >> 4) == iota((16, 128), 0), m_row, 0.0)
    expand = (iota((128, D), 0) & (PAD_HEADS - 1)) == (iota((128, D), 1) >> 6)
    expand = jnp.where(expand, 1.0, 0.0).astype(bf16)
    m_wide = two_part(dot_nn, m_row, expand)
    keys = m_wide * small_ref[3, 0:1, :]
    for k in range(SHARE):
        value = jnp.sum(jnp.where(iota((1, D), 1) == first + k, cls_f, 0.0), axis=-1, keepdims=True)
        for c in range(D // 128):
            lanes = slice(k * D + c * 128, k * D + (c + 1) * 128)
            out_ref[1, 0:1, lanes] = value * total[108 + c : 109 + c, :]
            out_ref[1, 1:2, lanes] = keys[k : k + 1, c * 128 : (c + 1) * 128]


def call(kernel, out_shape, scratch, specs, *operands):
    return pl.pallas_call(
        kernel,
        out_shape=out_shape,
        in_specs=specs,
        scratch_shapes=scratch,
        compiler_params=pltpu.CompilerParams(vmem_limit_bytes=VMEM_LIMIT),
        name=kernel.__name__,
    )(*operands)


def per_device(
    hidden,
    token_ids,
    passage_mask,
    labels,
    enc_weights,
    enc_gain,
    agg_weights,
    agg_gain,
    agg_cls,
    head_vector,
    score_bias,
):
    shape = jax.ShapeDtypeStruct
    whole = pl.BlockSpec(memory_space=pltpu.VMEM)
    scalar = pl.BlockSpec(memory_space=pltpu.SMEM)
    states = hidden.reshape(QUERIES, SLOTS, SEQ, D)
    width = 2 * D + 128
    pay_1, soft, z_rows = call(
        forward_kernel,
        (
            shape((PSG_DEV, LOCAL, width), bf16),
            shape((LOCAL * PAD_HEADS, SEQ), f32),
            shape((HEADS * LOCAL, D), bf16),
        ),
        [
            pltpu.VMEM((LOCAL, D), f32),
            pltpu.VMEM((D // 128, LOCAL * PAD_HEADS, 128), f32),
            pltpu.VMEM((3, D, D), bf16),
            pltpu.SemaphoreType.DMA((3,)),
        ],
        [whole, whole, whole, pl.BlockSpec(memory_space=pl.ANY)],
        states,
        token_ids.reshape(QUERIES, SLOTS, SEQ),
        passage_mask.reshape(QUERIES, SLOTS),
        enc_weights,
    )
    got = lax.all_to_all(pay_1, "psg", 0, 0, tiled=True)
    score, pay_2, query, gatt, gmix, zagg, pooled, small, m = call(
        backward_kernel,
        (
            shape((DOC_DEV, QUERIES, 128), f32),
            shape((PSG_DEV, ROWS + 32, 2 * HEADS * LOCAL), bf16),
            shape((GROUP, D), f32),
            shape((GROUP, D), f32),
            shape((GROUP, D), f32),
            shape((QUERIES * PAD_HEADS, D), bf16),
            shape((16, D), bf16),
            shape((4, QUERIES, D), f32),
            shape((QUERIES * PAD_HEADS, D), f32),
        ),
        [pltpu.VMEM((D // 128, LOCAL * PAD_HEADS, 128), f32)],
        [whole] * 10 + [scalar],
        got,
        states,
        soft,
        z_rows,
        enc_weights,
        enc_gain.reshape(1, D),
        agg_weights,
        agg_gain.reshape(1, D),
        agg_cls.reshape(1, D),
        head_vector.reshape(1, D),
        score_bias.reshape(1, 1),
    )
    everything = lax.all_to_all(score, "doc", 0, 0, tiled=True)
    recv = lax.all_to_all(pay_2, "psg", 0, 0, tiled=True)
    pay_3, loss = call(
        weights_kernel,
        (shape((DOC_DEV, PAY, 128), bf16), shape((1, 1), f32)),
        [pltpu.VMEM((DOC_DEV * PAY, 128), f32)],
        [whole] * 12,
        everything,
        score,
        labels.reshape(QUERIES, 1),
        recv,
        got,
        query,
        gatt,
        gmix,
        zagg,
        pooled,
        small,
        m,
    )
    shares = lax.all_to_all(pay_3, "doc", 0, 0, tiled=True)
    grads = call(
        finish_kernel,
        shape((2, 4, SHARE * D), f32),
        [],
        [whole] * 3,
        shares,
        small,
        agg_cls.reshape(1, D),
    )
    return (score[0, :, 0:1], loss.reshape(()), grads)


def solution(mesh):
    placed = (
        P(None, "doc", "psg", None, None),
        P(None, "doc", "psg", None),
        P(None, "doc", "psg"),
        P(),
        P(),
        P(),
        P(),
        P(),
        P(),
        P(),
        P(),
    )
    return jax.shard_map(
        per_device,
        mesh=mesh,
        in_specs=placed,
        out_specs=(P(None, "doc"), P(), P(None, None, ("psg", "doc"))),
        check_vma=False,
    )
```

```python
import jax
import jax.numpy as jnp
from jax import lax
from jax.experimental import pallas as pl
from jax.experimental.pallas import tpu as pltpu
from jax.sharding import PartitionSpec as P

HEADS = 12
HEAD = 64
D = 768
SEQ = 128
QUERIES = 8
SLOTS = 2
LOCAL = QUERIES * SLOTS
PSG_DEV = 8
DOC_DEV = 32
GROUP = PSG_DEV * LOCAL
ROWS = D // PSG_DEV
SHARE = ROWS // DOC_DEV
PAD_HEADS = 16
SCALE = HEAD ** (-0.5)

f32 = jnp.float32
bf16 = jnp.bfloat16


def dot_nn(a, b):
    return lax.dot_general(a, b, (((1,), (0,)), ((), ())), preferred_element_type=f32)


def dot_nt(a, b):
    return lax.dot_general(a, b, (((1,), (1,)), ((), ())), preferred_element_type=f32)


def dot_tn(a, b):
    return lax.dot_general(a, b, (((0,), (0,)), ((), ())), preferred_element_type=f32)


def halves(x):
    hi = x.astype(bf16)
    lo = (x - hi.astype(f32)).astype(bf16)
    return hi, lo


def two_part(dot, x, w):
    n = x.shape[0]
    both = dot(jnp.concatenate(halves(x), axis=0), w)
    return both[:n] + both[n:]


def iota(shape, dim):
    return lax.broadcasted_iota(jnp.int32, shape, dim)


def head_mask():
    return iota((PAD_HEADS, D), 0) == (iota((PAD_HEADS, D), 1) >> 6)


def spread(rows, mask):
    n = rows.shape[0]
    wide = jnp.where(mask[None], rows[:, None, :], 0.0)
    return wide.reshape(n * PAD_HEADS, D)


def fold(rows, mask):
    n = rows.shape[0] // PAD_HEADS
    wide = jnp.where(mask[None], rows.reshape(n, PAD_HEADS, D), 0.0)
    return jnp.sum(wide, axis=1)


QUAD = 4 * HEAD


def quad_mask():
    return iota((4, 1, QUAD), 0) == (iota((4, 1, QUAD), 2) >> 6)


def images(rows, w):
    n = rows.shape[0]
    parts = []
    for at in range(0, D, QUAD):
        wide = jnp.where(quad_mask(), rows[None, :, at : at + QUAD], 0.0).reshape(4 * n, QUAD)
        parts.append(two_part(dot_nt, wide, w[:, at : at + QUAD]))
    return jnp.concatenate(parts, axis=0)


def head_sums(rows, w):
    n = rows.shape[0] // HEADS
    parts = []
    for g, at in enumerate(range(0, D, QUAD)):
        out = two_part(dot_nn, rows[4 * n * g : 4 * n * (g + 1)], w[:, at : at + QUAD])
        parts.append(jnp.sum(jnp.where(quad_mask(), out.reshape(4, n, QUAD), 0.0), axis=0))
    return jnp.concatenate(parts, axis=1)


def norm_parts(x):
    center = x - jnp.mean(x, axis=-1, keepdims=True)
    rscale = lax.rsqrt(jnp.mean(center * center, axis=-1, keepdims=True) + 1e-05)
    return center * rscale, rscale


def norm_back(grad_out, gain, normed, rscale):
    grad_norm = grad_out * gain
    return rscale * (
        grad_norm
        - jnp.mean(grad_norm, axis=-1, keepdims=True)
        - normed * jnp.mean(grad_norm * normed, axis=-1, keepdims=True)
    )


def pick_rows(first):
    r = iota((ROWS, D), 0)
    want = first + SHARE * (r & (DOC_DEV - 1)) + (r >> 5)
    return jnp.where(iota((ROWS, D), 1) == want, 1.0, 0.0).astype(bf16)


def column(row):
    n = row.shape[1]
    wide = jnp.broadcast_to(row, (QUERIES, n))
    hit = iota((QUERIES, n), 0) == iota((QUERIES, n), 1)
    return jnp.sum(jnp.where(hit, wide, jnp.zeros_like(wide)), axis=1, keepdims=True)


def pack_columns(rows):
    half = ROWS // 2
    out = dot_nt(jnp.concatenate([pick_rows(ROWS * i) for i in range(PSG_DEV)], axis=0), rows)
    rest = out[:, 128:]
    high = [
        jnp.concatenate([rest[at : at + half], rest[at + half : at + ROWS]], axis=1)
        for at in range(0, D, ROWS)
    ]
    return out[:, :128].astype(bf16), jnp.concatenate(high, axis=0).astype(bf16)


def unpack_columns(low, high):
    both = jnp.concatenate([high, high], axis=0)
    keep = (iota((ROWS, 128), 0) < ROWS // 2) == (iota((ROWS, 128), 1) < 64)
    both = jnp.where(keep, both, jnp.zeros_like(both))
    return jnp.concatenate([low, both], axis=1)


def head_rows(rows):
    shape = (16, 1, D)
    head = iota(shape, 0)
    head = jnp.where(head < HEADS, head, head - 4)
    keep = head == (iota(shape, 2) >> 6)
    return jnp.where(keep, rows[None], jnp.zeros_like(rows)[None]).reshape(16 * LOCAL, D)


def put(out_s, at, rows, pay):
    for k in range(SHARE):
        for c in range(D // 128):
            out_s[pl.ds(at + k * (D // 128) + c, DOC_DEV, stride=pay), :] = rows[
                k * DOC_DEV : (k + 1) * DOC_DEV, c * 128 : (c + 1) * 128
            ]


def heads_at(p):
    return slice(p * PAD_HEADS, (p + 1) * PAD_HEADS)


def to_scratch(rows, scratch):
    for c in range(D // 128):
        scratch[c, : HEADS * LOCAL, :] = rows[:, c * 128 : (c + 1) * 128]
        scratch[c, HEADS * LOCAL :, :] = jnp.zeros(((PAD_HEADS - HEADS) * LOCAL, 128), f32)


def against_rows(scratch, rows_of):
    parts = [None] * LOCAL
    for q in range(QUERIES):
        rows = rows_of(q)
        for sl in range(SLOTS):
            p = sl * QUERIES + q
            x = [scratch[c, pl.ds(p, PAD_HEADS, stride=LOCAL), :] for c in range(D // 128)]
            left = jnp.concatenate(halves(jnp.concatenate(x, axis=1)), axis=0)
            out = dot_nt(left, rows[sl * SEQ : (sl + 1) * SEQ])
            parts[p] = out[:PAD_HEADS] + out[PAD_HEADS:]
    return jnp.concatenate(parts, axis=0)


def sum_rows(x, rows_of):
    hi, lo = halves(x)
    parts = [None] * LOCAL
    blank = jnp.zeros((PAD_HEADS, SEQ), bf16)
    for q in range(QUERIES):
        a, b = heads_at(q), heads_at(QUERIES + q)
        left = [[hi[a], blank], [blank, hi[b]], [lo[a], blank], [blank, lo[b]]]
        left = jnp.concatenate([jnp.concatenate(row, axis=1) for row in left], axis=0)
        out = dot_nn(left, rows_of(q))
        parts[q] = out[0:16] + out[32:48]
        parts[QUERIES + q] = out[16:32] + out[48:64]
    return parts


def by_head(parts, scratch):
    for p, part in enumerate(parts):
        for c in range(D // 128):
            scratch[c, pl.ds(p, PAD_HEADS, stride=LOCAL), :] = part[:, c * 128 : (c + 1) * 128]
    return jnp.concatenate([scratch[c, : HEADS * LOCAL, :] for c in range(D // 128)], axis=1)


def forward_kernel(
    top_ref, w_ref, hid_ref, ids_ref, mask_ref, wv_ref, pay_ref, soft_ref, z_ref, h0_s, qk_s, z_s
):
    for sl in range(SLOTS):
        for q in range(QUERIES):
            p = sl * QUERIES + q
            h0_s[p : p + 1, :] = top_ref[q, sl].astype(f32)[0:1, :]
    h0 = h0_s[...].astype(bf16)
    query = dot_nn(h0, w_ref[0][...]) * SCALE
    to_scratch(images(query, w_ref[1].ready()), qk_s)
    rows_of = lambda q: hid_ref[q][...].reshape(SLOTS * SEQ, D)
    logits = against_rows(qk_s, rows_of)
    valid = [
        jnp.broadcast_to(ids_ref[q, sl : sl + 1, :], (PAD_HEADS, SEQ))
        for sl in range(SLOTS)
        for q in range(QUERIES)
    ]
    valid = jnp.concatenate(valid, axis=0) != 0
    logits = jnp.where(valid, logits, -1e30)
    peak = jnp.max(logits, axis=-1, keepdims=True)
    raw = jnp.where(valid, jnp.exp(logits - peak), 0.0)
    soft = raw / jnp.sum(raw, axis=-1, keepdims=True)
    soft_ref.send(soft)
    z = by_head(sum_rows(soft, rows_of), z_s)
    z_ref.send(z.astype(bf16))
    attended = head_sums(z, wv_ref[2].ready())
    keep = [
        jnp.broadcast_to(column(mask_ref[sl : sl + 1, :]), (QUERIES, 128)) for sl in range(SLOTS)
    ]
    keep = jnp.where(jnp.concatenate(keep, axis=0) != 0, 1.0, 0.0).astype(bf16)
    row = jnp.concatenate([h0, attended.astype(bf16), keep], axis=1)
    for i in range(PSG_DEV):
        pay_ref[i] = row


def class_kernel(after_ref, vec_ref, wa_ref, out_ref):
    cls_f = vec_ref[3:4, :]
    cls_8 = jnp.broadcast_to(cls_f, (QUERIES, D)).astype(bf16)
    cls_query = dot_nn(cls_8, wa_ref[0][...])
    kq = two_part(dot_nt, jnp.where(head_mask(), cls_query[0:1], 0.0), wa_ref[1][...])
    out_ref[0] = jnp.broadcast_to(cls_query[0:1], (PAD_HEADS, D))
    out_ref[1] = kq
    cls_logit = jnp.sum(kq * cls_f, axis=-1, keepdims=True) * SCALE
    out_ref[2] = jnp.broadcast_to(cls_logit, (PAD_HEADS, D))


def score_kernel(
    got_ref,
    we_ref,
    vec_ref,
    class_ref,
    wa_ref,
    score_ref,
    own_ref,
    normed_ref,
    rscale_ref,
    zagg_ref,
    soft_ref,
    small_ref,
):
    got = got_ref[...].reshape(GROUP, 2 * D + 128)
    h0 = got[:, :D]
    att = got[:, D : 2 * D]
    keep = got[:, 2 * D :]
    lane_one = jnp.where(iota((16, 128), 1) == 0, 1.0, 0.0).astype(bf16)
    present = dot_nt(lane_one, keep)[0:1]
    shape3 = (HEADS, QUERIES, GROUP)
    valid = ((iota(shape3, 2) & (QUERIES - 1)) == iota(shape3, 1)) & (present[None] > 0.5)
    normed_e, rscale_e = norm_parts(h0.astype(f32) + dot_nn(att, we_ref[3][...]))
    normed_ref.send(normed_e)
    rscale_ref.send(jnp.broadcast_to(rscale_e, (GROUP, 128)))
    passage = (normed_e * vec_ref[0:1, :]).astype(bf16)
    cls_f = vec_ref[3:4, :]
    logit = two_part(dot_nt, class_ref[1], passage)[:HEADS] * SCALE
    cls_logit = class_ref[2][:HEADS, 0:1]
    logit3 = jnp.where(valid, logit[:, None, :], -1e30)
    cls_logit = cls_logit[:, None, :]
    peak = jnp.maximum(jnp.max(logit3, axis=-1, keepdims=True), cls_logit)
    raw = jnp.where(valid, jnp.exp(logit3 - peak), 0.0)
    cls_raw = jnp.exp(cls_logit - peak)
    total = jnp.sum(raw, axis=-1, keepdims=True) + cls_raw
    soft = (raw / total).reshape(HEADS * QUERIES, GROUP)
    cls_prob = (cls_raw / total).reshape(HEADS * QUERIES, 1)
    soft_ref[0] = soft
    soft_ref[1] = jnp.broadcast_to(cls_prob, (HEADS * QUERIES, GROUP))
    soft_ref.send()
    zagg = two_part(dot_nn, soft, passage) + cls_prob * cls_f
    zagg_ref.send(zagg)
    pooled = head_sums(zagg, wa_ref[2].ready())
    small_ref[2] = pooled
    pooled_b = jnp.concatenate([pooled, jnp.zeros_like(pooled)], axis=0).astype(bf16)
    normed_a, rscale_a = norm_parts(cls_f + dot_nn(pooled_b, wa_ref[3][...])[:QUERIES])
    small_ref[0] = normed_a
    small_ref[1] = jnp.broadcast_to(rscale_a, (QUERIES, D))
    small_ref.send()
    score = jnp.sum(normed_a * vec_ref[1:2, :] * vec_ref[2:3, :], axis=-1, keepdims=True)
    score = jnp.broadcast_to(score + vec_ref[4:5, 0:1], (QUERIES, 128))
    own_ref.send(score)
    diagonal = iota((QUERIES, 128), 0) == iota((QUERIES, 128), 1)
    row = jnp.sum(jnp.where(diagonal, score, 0.0), axis=0, keepdims=True)
    for j in range(DOC_DEV):
        score_ref[j] = row


def backward_kernel(
    z_ref,
    vec_ref,
    small_ref,
    wa_ref,
    zagg_ref,
    normed_ref,
    soft_ref,
    class_ref,
    rscale_ref,
    we_ref,
    hid_ref,
    soft_e_ref,
    wk_ref,
    pay_ref,
    gatt_ref,
    gmix_ref,
    gpv_ref,
    glogit_ref,
    back_ref,
    wv_s,
    u_s,
):
    half = ROWS // 2

    def pay(at, rows):
        low, high = pack_columns(rows.astype(bf16))
        for i in range(PSG_DEV):
            pay_ref[i, at : at + ROWS, :] = low[i * ROWS : (i + 1) * ROWS]
            pay_ref[i, at + ROWS : at + ROWS + half, :] = high[i * half : (i + 1) * half]

    z_ref.ready()
    for fetched in (zagg_ref, normed_ref, soft_ref, class_ref, rscale_ref):
        fetched.begin()
    we_ref[3].begin()
    we_ref[2].begin()
    pay(0, z_ref[...])
    me = lax.axis_index("psg")
    head = jnp.broadcast_to(vec_ref[2:3, :], (QUERIES, D))
    gmix_a = norm_back(head, vec_ref[1:2, :], small_ref[0], small_ref[1][:, 0:1])
    back_ref[1] = gmix_a
    gmix_a16 = jnp.concatenate([gmix_a, jnp.zeros_like(gmix_a)], axis=0).astype(bf16)
    wa_ref[2].ready()
    for q in range(QUERIES):
        hid_ref[q].begin()
    soft_e_ref.begin()
    wk_ref[1].begin()
    gpool = dot_nt(gmix_a16, wa_ref[3][...])[:QUERIES]
    back_ref[0] = gpool
    back_ref.send()
    gpv = images(gpool, wa_ref[2].ready())
    gpv_ref.send(gpv)
    base = jnp.sum(gpv * zagg_ref[...], axis=-1, keepdims=True)
    normed_e = normed_ref[...]
    gain_e = vec_ref[0:1, :]
    passage = (normed_e * gain_e).astype(bf16)
    along = two_part(dot_nt, gpv, passage)
    soft = soft_ref[0]
    glogit = soft * (along - base) * SCALE
    glogit_ref[0] = glogit
    glogit_ref[1] = jnp.broadcast_to(base, (HEADS * QUERIES, GROUP))
    glogit_ref.send()
    kq_wide = jnp.broadcast_to(class_ref[1][:HEADS, None, :], (HEADS, QUERIES, D))
    kq_wide = kq_wide.reshape(HEADS * QUERIES, D)
    left = jnp.concatenate([glogit, soft], axis=0).astype(bf16)
    right = jnp.concatenate([kq_wide, gpv], axis=0).astype(bf16)
    gpass = dot_tn(left, right)
    gmix_e = norm_back(gpass, gain_e, normed_e, rscale_ref[:, 0:1])
    gmix_ref.send(gmix_e)
    gatt_ref.send(dot_nt(gmix_e.astype(bf16), we_ref[3][...]))
    mine = gatt_ref[pl.ds(pl.multiple_of(me * LOCAL, LOCAL), LOCAL), :]
    to_scratch(images(mine, we_ref[2].ready()), wv_s)
    rows_of = lambda q: hid_ref[q][...].reshape(SLOTS * SEQ, D)
    along_e = against_rows(wv_s, rows_of)
    soft_e = soft_e_ref[...]
    base_e = jnp.sum(soft_e * along_e, axis=-1, keepdims=True)
    u = by_head(sum_rows(soft_e * (along_e - base_e) * SCALE, rows_of), u_s)
    gquery = head_sums(u, wk_ref[1].ready()).astype(bf16)
    for i in range(PSG_DEV):
        for c in range(D // 128):
            pay_ref[i, 288 + 16 * c : 304 + 16 * c, :] = gquery[:, c * 128 : (c + 1) * 128]
    pay(144, u)


EARLY = 64
LATE = 56


def early_kernel(
    all_ref,
    own_ref,
    labels_ref,
    gatt_ref,
    gmix_ref,
    got_ref,
    zagg_ref,
    back_ref,
    small_ref,
    vec_ref,
    soft_ref,
    gpv_ref,
    glogit_ref,
    normed_ref,
    we_ref,
    wa_ref,
    pay_ref,
    loss_ref,
    g_ref,
    right_ref,
    left_ref,
    score_ref,
    out_s,
):
    diagonal = iota((QUERIES, 128), 0) == iota((QUERIES, 128), 1)
    row = jnp.sum(jnp.where(diagonal, own_ref[...], 0.0), axis=0, keepdims=True)
    score_ref[...] = row[:, :QUERIES]
    me = lax.axis_index("psg")
    doc = lax.axis_index("doc")
    everything = all_ref[...]
    labels = labels_ref[...]
    lane_labels = jnp.concatenate([labels, jnp.full((1, 120), -1, jnp.int32)], axis=1)
    peak = jnp.max(everything, axis=0)
    total = jnp.sum(jnp.exp(everything - peak[None]), axis=0)
    hits = iota((DOC_DEV, 1, 128), 0) == lane_labels[None]
    label_score = jnp.sum(jnp.where(hits, everything, 0.0), axis=0)
    losses = jnp.log(total) + peak - label_score
    losses = jnp.where(iota((1, 128), 1) < QUERIES, losses, 0.0)
    loss_ref[...] = jnp.sum(losses, axis=1, keepdims=True) / QUERIES
    own_hit = jnp.where(column(labels) == doc, 1.0, 0.0)
    g8 = (jnp.exp(own_ref[:, 0:1] - column(peak)) / column(total) - own_hit) / QUERIES
    g8 = jnp.broadcast_to(g8, (QUERIES, D))
    g16 = jnp.concatenate([g8, g8], axis=0)
    g_ref[...] = g16
    g_group = jnp.concatenate([g16] * PSG_DEV, axis=0)
    g_heads = jnp.concatenate([g8] * HEADS, axis=0)
    pick = pick_rows(me * ROWS)
    got = got_ref[...].reshape(GROUP, 2 * D + 128)
    left_ref[...] = dot_nt(pick, got[:, :D]).astype(bf16)
    right_ref[1] = (gatt_ref[...] * g_group).astype(bf16)
    att_t = dot_nt(pick, got[:, D : 2 * D]).astype(bf16)
    put(out_s, 0, dot_nn(att_t, (gmix_ref[...] * g_group).astype(bf16)), EARLY)
    zagg_t = dot_nt(pick, zagg_ref[...].astype(bf16)).astype(bf16)
    shape3 = (HEADS, 1, D)
    own_head = iota(shape3, 0) == (iota(shape3, 2) >> 6)
    gpool = jnp.where(own_head, (back_ref[0] * g8)[None], 0.0).reshape(HEADS * QUERIES, D)
    put(out_s, 18, dot_nn(zagg_t, gpool.astype(bf16)), EARLY)
    blank = jnp.zeros((120, D), f32)
    pooled = jnp.concatenate([small_ref[2], blank], axis=0).astype(bf16)
    pooled_t = dot_nt(pick, pooled).astype(bf16)
    gmix_a = jnp.concatenate([back_ref[1] * g8, blank], axis=0).astype(bf16)
    put(out_s, 36, dot_nn(pooled_t, gmix_a), EARLY)
    cls_f = vec_ref[3:4, :]
    along = jnp.sum(gpv_ref[...] * cls_f, axis=-1, keepdims=True)
    cls_glogit = soft_ref[1][:, 0:1] * (along - glogit_ref[1][:, 0:1]) * SCALE
    passage = (normed_ref[...] * vec_ref[0:1, :]).astype(bf16)
    m = two_part(dot_nn, glogit_ref[0], passage) + cls_glogit * cls_f
    m_sum = jnp.sum((m * g_heads).reshape(HEADS, QUERIES, D), axis=1)
    m_sum = jnp.concatenate([m_sum, jnp.zeros((PAD_HEADS - HEADS, D), f32)], axis=0)
    right_ref[0] = (dot_nn(got[:, :D], we_ref[0][...]) * g_group).astype(bf16)
    qvec = fold(two_part(dot_nn, m_sum, wa_ref[1][...]), head_mask())
    for c in range(D // 128):
        out_s[pl.ds(54 + c, DOC_DEV, stride=EARLY), :] = jnp.broadcast_to(
            qvec[:, c * 128 : (c + 1) * 128], (DOC_DEV, 128)
        )
    m_hi, m_lo = halves(jnp.concatenate([m_sum] * 8, axis=0))
    m_t = dot_nt(pick, m_hi) + dot_nt(pick, m_lo)
    lane_k = iota((DOC_DEV, 128), 1) >> 4
    m_row = jnp.zeros((DOC_DEV, 128), f32)
    for k in range(SHARE):
        m_row = jnp.where(lane_k == k, m_t[k * DOC_DEV : (k + 1) * DOC_DEV], m_row)
    out_s[pl.ds(60, DOC_DEV, stride=EARLY), :] = m_row
    for r in range(61, EARLY):
        out_s[pl.ds(r, DOC_DEV, stride=EARLY), :] = jnp.zeros((DOC_DEV, 128), f32)
    pay_ref[...] = out_s[...].astype(bf16).reshape(DOC_DEV, EARLY, 128)


def late_kernel(recv_ref, left_ref, right_ref, g_ref, early_ref, pay_ref, out_s):
    g16 = g_ref[...]
    gq = []
    gk = jnp.zeros((ROWS, D), f32)
    gv = jnp.zeros((ROWS, D), f32)
    for s in range(PSG_DEV):
        at = slice(s * LOCAL, (s + 1) * LOCAL)
        block = recv_ref[s]
        gv = gv + dot_nn(unpack_columns(block[:96], block[96:144]), head_rows(right_ref[1, at, :]))
        gk = gk + dot_nn(
            unpack_columns(block[144:240], block[240:288]), head_rows(right_ref[0, at, :])
        )
        parts = [block[288 + 16 * c : 304 + 16 * c] for c in range(D // 128)]
        gq.append((jnp.concatenate(parts, axis=1).astype(f32) * g16).astype(bf16))
    put(out_s, 0, dot_nn(left_ref[...], jnp.concatenate(gq, axis=0)), LATE)
    put(out_s, 18, gk, LATE)
    put(out_s, 36, gv, LATE)
    for r in range(54, LATE):
        out_s[pl.ds(r, DOC_DEV, stride=LATE), :] = jnp.zeros((DOC_DEV, 128), f32)
    late = out_s[...].astype(bf16).reshape(DOC_DEV, LATE, 128)
    pay_ref[...] = jnp.concatenate([early_ref[...], late], axis=1)


def finish_kernel(recv_ref, class_ref, vec_ref, out_ref):
    first = lax.axis_index("psg") * ROWS + lax.axis_index("doc") * SHARE
    total = recv_ref[0].astype(f32)
    for j in range(1, DOC_DEV):
        total = total + recv_ref[j].astype(f32)
    place = [
        (EARLY, 0, 0),
        (EARLY + 18, 0, 1),
        (EARLY + 36, 0, 2),
        (0, 0, 3),
        (18, 1, 2),
        (36, 1, 3),
    ]
    for at, layer, proj in place:
        for r in range(18):
            out_ref[layer, proj : proj + 1, r * 128 : (r + 1) * 128] = total[at + r : at + r + 1, :]
    cls_f = vec_ref[3:4, :]
    m_row = jnp.broadcast_to(total[60:61, :], (16, 128))
    m_row = jnp.where((iota((16, 128), 1) >> 4) == iota((16, 128), 0), m_row, 0.0)
    expand = (iota((128, D), 0) & (PAD_HEADS - 1)) == (iota((128, D), 1) >> 6)
    expand = jnp.where(expand, 1.0, 0.0).astype(bf16)
    keys = two_part(dot_nn, m_row, expand) * class_ref[0, 0:1, :]
    for k in range(SHARE):
        value = jnp.sum(jnp.where(iota((1, D), 1) == first + k, cls_f, 0.0), axis=-1, keepdims=True)
        for c in range(D // 128):
            lanes = slice(k * D + c * 128, k * D + (c + 1) * 128)
            out_ref[1, 0:1, lanes] = value * total[54 + c : 55 + c, :]
            out_ref[1, 1:2, lanes] = keys[k : k + 1, c * 128 : (c + 1) * 128]


WHOLE = pl.BlockSpec(memory_space=pltpu.VMEM)
SCALAR = pl.BlockSpec(memory_space=pltpu.SMEM)
FAR = pl.BlockSpec(memory_space=pl.ANY)


TOP = "top"


class Fetched:
    def __init__(self, src, dst, sem):
        self.copy = pltpu.make_async_copy(src, dst, sem)
        self.dst = dst
        self.started = False
        self.waiting = True

    def begin(self):
        if not self.started:
            self.copy.start()
            self.started = True

    def ready(self):
        self.begin()
        if self.waiting:
            self.copy.wait()
            self.waiting = False
        return self.dst

    def __getitem__(self, index):
        return self.ready()[index]


class Sent:
    def __init__(self, buf, dst, sem):
        self.buf = buf
        self.copy = pltpu.make_async_copy(buf, dst, sem)
        self.going = False

    def __getitem__(self, index):
        return self.buf[index]

    def __setitem__(self, index, value):
        self.buf[index] = value

    def send(self, value=None):
        if value is not None:
            self.buf[...] = value
        self.copy.start()
        self.going = True


def call(kernel, out_shape, scratch, operands, limit=56, first=99):
    single = not isinstance(out_shape, tuple)
    out_shape = (out_shape,) if single else out_shape
    specs, values, plans, buffers = [], [], [], []
    for operand in operands:
        parts = None
        spec = FAR
        if isinstance(operand, tuple):
            if isinstance(operand[0], pl.BlockSpec):
                spec, operand = operand
            else:
                operand, parts = operand
        if spec is FAR:
            operand = pltpu.with_memory_space_constraint(operand, pltpu.HBM)
            plans.append((len(values), parts))
            size = operand.shape if parts is None else (len(parts),) + operand.shape[1:]
            if parts is TOP:
                size = operand.shape[:2] + (16,) + operand.shape[3:]
            buffers.append(pltpu.VMEM(size, operand.dtype))
        specs.append(spec)
        values.append(operand)
    n_sems = sum(1 if parts in (None, TOP) else len(parts) for _, parts in plans)
    n_in, n_buf, n_out = len(values), len(buffers), len(out_shape)

    def body(*refs):
        ins = list(refs[:n_in])
        outs = refs[n_in : n_in + n_out]
        own = refs[n_in + n_out : -1 - n_buf - n_out]
        bufs = refs[-1 - n_buf - n_out : -1 - n_out]
        out_bufs = refs[-1 - n_out : -1]
        sems = refs[-1]
        started = []
        for (at, parts), buf in zip(plans, bufs):
            if parts is None or parts is TOP:
                ref = ins[at] if parts is None else ins[at].at[:, :, pl.ds(0, 16), :]
                ins[at] = Fetched(ref, buf, sems.at[len(started)])
                started.append(ins[at])
            else:
                ref, ins[at] = ins[at], {}
                for n, part in enumerate(parts):
                    ins[at][part] = Fetched(ref.at[part], buf.at[n], sems.at[len(started)])
                    started.append(ins[at][part])
        for fetched in started[:first]:
            fetched.begin()
        sent = [Sent(*both, sems.at[n_sems + n]) for n, both in enumerate(zip(out_bufs, outs))]
        kernel(*ins, *sent, *own)
        for out in sent:
            if not out.going:
                out.send()
        for fetched in started:
            fetched.ready()
        for out in sent:
            out.copy.wait()

    outs = pl.pallas_call(
        body,
        out_shape=tuple(pltpu.HBM(leaf.shape, leaf.dtype) for leaf in out_shape),
        in_specs=specs,
        out_specs=tuple(FAR for leaf in out_shape),
        scratch_shapes=list(scratch)
        + buffers
        + [pltpu.VMEM(leaf.shape, leaf.dtype) for leaf in out_shape]
        + [pltpu.SemaphoreType.DMA((n_sems + n_out,))],
        compiler_params=pltpu.CompilerParams(vmem_limit_bytes=limit * 1024 * 1024),
        name=kernel.__name__,
    )(*values)
    return outs[0] if single else outs


def per_device(
    hidden,
    token_ids,
    passage_mask,
    labels,
    enc_weights,
    enc_gain,
    agg_weights,
    agg_gain,
    agg_cls,
    head_vector,
    score_bias,
):
    shape = jax.ShapeDtypeStruct
    states = hidden.reshape(QUERIES, SLOTS, SEQ, D)
    vectors = [enc_gain, agg_gain, head_vector, agg_cls.astype(f32), jnp.full((D,), score_bias)]
    vectors = jnp.stack(vectors + [jnp.zeros((D,), f32)] * 3)
    head_scratch = pltpu.VMEM((D // 128, LOCAL * PAD_HEADS, 128), f32)
    pairs = HEADS * QUERIES
    group = shape((GROUP, D), f32)
    pay_1, soft_e, z_rows = call(
        forward_kernel,
        (
            shape((PSG_DEV, LOCAL, 2 * D + 128), bf16),
            shape((LOCAL * PAD_HEADS, SEQ), f32),
            shape((HEADS * LOCAL, D), bf16),
        ),
        [pltpu.VMEM((LOCAL, D), f32), head_scratch, head_scratch],
        (
            (states, TOP),
            (enc_weights, (0, 1)),
            (states, tuple(range(QUERIES))),
            token_ids.reshape(QUERIES, SLOTS, SEQ),
            passage_mask.transpose(1, 2, 0).reshape(SLOTS, QUERIES),
            (enc_weights, (2,)),
        ),
    )
    got = lax.all_to_all(pay_1, "psg", 0, 0, tiled=True)
    class_rows = call(
        class_kernel,
        shape((3, PAD_HEADS, D), f32),
        [],
        (z_rows, vectors, (agg_weights, (0, 1))),
    )
    score, own, normed, rscale, zagg, soft, small = call(
        score_kernel,
        (
            shape((DOC_DEV, 1, 128), f32),
            shape((QUERIES, 128), f32),
            group,
            shape((GROUP, 128), f32),
            shape((pairs, D), f32),
            shape((2, pairs, GROUP), f32),
            shape((3, QUERIES, D), f32),
        ),
        [],
        ((WHOLE, got), (enc_weights, (3,)), vectors, class_rows, (agg_weights, (2, 3))),
        limit=24,
    )
    everything = lax.all_to_all(score, "doc", 0, 0, tiled=True)
    pay_2, gatt, gmix, gpv, glogit, back = call(
        backward_kernel,
        (
            shape((PSG_DEV, 384, 128), bf16),
            group,
            group,
            shape((pairs, D), f32),
            shape((2, pairs, GROUP), f32),
            shape((2, QUERIES, D), f32),
        ),
        [head_scratch, head_scratch],
        (
            z_rows,
            vectors,
            small,
            (agg_weights, (3, 2)),
            zagg,
            normed,
            soft,
            class_rows,
            rscale,
            (enc_weights, (3, 2)),
            (states, tuple(range(QUERIES))),
            soft_e,
            (enc_weights, (1,)),
        ),
    )
    recv = lax.all_to_all(pay_2, "psg", 0, 0, tiled=True)
    early, loss, g16, right, left, scores = call(
        early_kernel,
        (
            shape((DOC_DEV, EARLY, 128), bf16),
            shape((1, 1), f32),
            shape((LOCAL, D), f32),
            shape((2, GROUP, D), bf16),
            shape((ROWS, GROUP), bf16),
            shape((1, QUERIES), f32),
        ),
        [pltpu.VMEM((DOC_DEV * EARLY, 128), f32)],
        (
            everything,
            own,
            labels.reshape(1, QUERIES),
            gatt,
            gmix,
            got,
            zagg,
            back,
            small,
            vectors,
            soft,
            gpv,
            glogit,
            normed,
            (enc_weights, (0,)),
            (agg_weights, (1,)),
        ),
    )
    pay_3 = call(
        late_kernel,
        shape((DOC_DEV, EARLY + LATE, 128), bf16),
        [pltpu.VMEM((DOC_DEV * LATE, 128), f32)],
        ((WHOLE, recv), left, right, g16, early),
        limit=24,
    )
    shares = lax.all_to_all(pay_3, "doc", 0, 0, tiled=True)
    weight_grads = call(
        finish_kernel,
        shape((2, 4, SHARE * D), f32),
        [],
        ((WHOLE, shares), class_rows, vectors),
        limit=16,
    )
    return (scores.reshape(QUERIES, 1), loss.reshape(()), weight_grads)


def solution(mesh):
    placed = (
        P(None, "doc", "psg", None, None),
        P(None, "doc", "psg", None),
        P(None, "doc", "psg"),
        P(),
        P(),
        P(),
        P(),
        P(),
        P(),
        P(),
        P(),
    )
    return jax.shard_map(
        per_device,
        mesh=mesh,
        in_specs=placed,
        out_specs=(P(None, "doc"), P(), P(None, None, ("psg", "doc"))),
        check_vma=False,
    )
```

```python
import jax
import jax.numpy as jnp
from jax import lax
from jax.experimental import pallas as pl
from jax.experimental.pallas import tpu as pltpu
from jax.sharding import PartitionSpec as P

HEADS = 12
HEAD = 64
D = 768
SEQ = 128
QUERIES = 8
SLOTS = 2
LOCAL = QUERIES * SLOTS
PSG_DEV = 8
DOC_DEV = 32
GROUP = PSG_DEV * LOCAL
ROWS = D // PSG_DEV
SHARE = ROWS // DOC_DEV
PAD_HEADS = 16
SCALE = HEAD ** (-0.5)

f32 = jnp.float32
bf16 = jnp.bfloat16


def dot_nn(a, b):
    return lax.dot_general(a, b, (((1,), (0,)), ((), ())), preferred_element_type=f32)


def dot_nt(a, b):
    return lax.dot_general(a, b, (((1,), (1,)), ((), ())), preferred_element_type=f32)


def dot_tn(a, b):
    return lax.dot_general(a, b, (((0,), (0,)), ((), ())), preferred_element_type=f32)


def halves(x):
    hi = x.astype(bf16)
    lo = (x - hi.astype(f32)).astype(bf16)
    return hi, lo


def two_part(dot, x, w):
    n = x.shape[0]
    both = dot(jnp.concatenate(halves(x), axis=0), w)
    return both[:n] + both[n:]


def iota(shape, dim):
    return lax.broadcasted_iota(jnp.int32, shape, dim)


def head_mask():
    return iota((PAD_HEADS, D), 0) == (iota((PAD_HEADS, D), 1) >> 6)


def spread(rows, mask):
    n = rows.shape[0]
    wide = jnp.where(mask[None], rows[:, None, :], 0.0)
    return wide.reshape(n * PAD_HEADS, D)


def fold(rows, mask):
    n = rows.shape[0] // PAD_HEADS
    wide = jnp.where(mask[None], rows.reshape(n, PAD_HEADS, D), 0.0)
    return jnp.sum(wide, axis=1)


QUAD = 4 * HEAD


def quad_mask():
    return iota((4, 1, QUAD), 0) == (iota((4, 1, QUAD), 2) >> 6)


def images(rows, w):
    n = rows.shape[0]
    parts = []
    for at in range(0, D, QUAD):
        wide = jnp.where(quad_mask(), rows[None, :, at : at + QUAD], 0.0).reshape(4 * n, QUAD)
        parts.append(two_part(dot_nt, wide, w[:, at : at + QUAD]))
    return jnp.concatenate(parts, axis=0)


def head_sums(rows, w):
    n = rows.shape[0] // HEADS
    parts = []
    for g, at in enumerate(range(0, D, QUAD)):
        out = two_part(dot_nn, rows[4 * n * g : 4 * n * (g + 1)], w[:, at : at + QUAD])
        parts.append(jnp.sum(jnp.where(quad_mask(), out.reshape(4, n, QUAD), 0.0), axis=0))
    return jnp.concatenate(parts, axis=1)


def norm_parts(x):
    center = x - jnp.mean(x, axis=-1, keepdims=True)
    rscale = lax.rsqrt(jnp.mean(center * center, axis=-1, keepdims=True) + 1e-05)
    return center * rscale, rscale


def norm_back(grad_out, gain, normed, rscale):
    grad_norm = grad_out * gain
    return rscale * (
        grad_norm
        - jnp.mean(grad_norm, axis=-1, keepdims=True)
        - normed * jnp.mean(grad_norm * normed, axis=-1, keepdims=True)
    )


def pick_rows(first):
    me = lax.axis_index("doc")
    r = iota((ROWS, D), 0)
    place = (((r & 7) << 2) + ((r >> 3) & 3)) ^ (me & 3)
    want = first + SHARE * place + (r >> 5)
    return jnp.where(iota((ROWS, D), 1) == want, 1.0, 0.0).astype(bf16)


def column(row):
    n = row.shape[1]
    wide = jnp.broadcast_to(row, (QUERIES, n))
    hit = iota((QUERIES, n), 0) == iota((QUERIES, n), 1)
    return jnp.sum(jnp.where(hit, wide, jnp.zeros_like(wide)), axis=1, keepdims=True)


def pack_columns(rows):
    half = ROWS // 2
    out = dot_nt(jnp.concatenate([pick_rows(ROWS * i) for i in range(PSG_DEV)], axis=0), rows)
    rest = out[:, 128:]
    high = [
        jnp.concatenate([rest[at : at + half], rest[at + half : at + ROWS]], axis=1)
        for at in range(0, D, ROWS)
    ]
    return out[:, :128].astype(bf16), jnp.concatenate(high, axis=0).astype(bf16)


def unpack_columns(low, high):
    both = jnp.concatenate([high, high], axis=0)
    keep = (iota((ROWS, 128), 0) < ROWS // 2) == (iota((ROWS, 128), 1) < 64)
    both = jnp.where(keep, both, jnp.zeros_like(both))
    return jnp.concatenate([low, both], axis=1)


def head_rows(rows):
    shape = (16, 1, D)
    head = iota(shape, 0)
    head = jnp.where(head < HEADS, head, head - 4)
    keep = head == (iota(shape, 2) >> 6)
    return jnp.where(keep, rows[None], jnp.zeros_like(rows)[None]).reshape(16 * LOCAL, D)


def put(out_s, at, rows, pay):
    for k in range(SHARE):
        for c in range(D // 128):
            out_s[pl.ds(at + k * (D // 128) + c, DOC_DEV, stride=pay), :] = rows[
                k * DOC_DEV : (k + 1) * DOC_DEV, c * 128 : (c + 1) * 128
            ]


def heads_at(p):
    return slice(p * PAD_HEADS, (p + 1) * PAD_HEADS)


def to_scratch(rows, scratch):
    for c in range(D // 128):
        scratch[c, : HEADS * LOCAL, :] = rows[:, c * 128 : (c + 1) * 128]
        scratch[c, HEADS * LOCAL :, :] = jnp.zeros(((PAD_HEADS - HEADS) * LOCAL, 128), f32)


def against_rows(scratch, rows_of):
    parts = [None] * LOCAL
    for q in range(QUERIES):
        rows = rows_of(q)
        for sl in range(SLOTS):
            p = sl * QUERIES + q
            x = [scratch[c, pl.ds(p, PAD_HEADS, stride=LOCAL), :] for c in range(D // 128)]
            left = jnp.concatenate(halves(jnp.concatenate(x, axis=1)), axis=0)
            out = dot_nt(left, rows[sl * SEQ : (sl + 1) * SEQ])
            parts[p] = out[:PAD_HEADS] + out[PAD_HEADS:]
    return jnp.concatenate(parts, axis=0)


def sum_rows(x, rows_of):
    hi, lo = halves(x)
    parts = [None] * LOCAL
    blank = jnp.zeros((PAD_HEADS, SEQ), bf16)
    for q in range(QUERIES):
        a, b = heads_at(q), heads_at(QUERIES + q)
        left = [[hi[a], blank], [blank, hi[b]], [lo[a], blank], [blank, lo[b]]]
        left = jnp.concatenate([jnp.concatenate(row, axis=1) for row in left], axis=0)
        out = dot_nn(left, rows_of(q))
        parts[q] = out[0:16] + out[32:48]
        parts[QUERIES + q] = out[16:32] + out[48:64]
    return parts


def by_head(parts, scratch):
    for p, part in enumerate(parts):
        for c in range(D // 128):
            scratch[c, pl.ds(p, PAD_HEADS, stride=LOCAL), :] = part[:, c * 128 : (c + 1) * 128]
    return jnp.concatenate([scratch[c, : HEADS * LOCAL, :] for c in range(D // 128)], axis=1)


def forward_kernel(
    top_ref, w_ref, hid_ref, ids_ref, mask_ref, wv_ref, pay_ref, soft_ref, z_ref, h0_s, qk_s, z_s
):
    for sl in range(SLOTS):
        for q in range(QUERIES):
            p = sl * QUERIES + q
            h0_s[p : p + 1, :] = top_ref[q, sl].astype(f32)[0:1, :]
    h0 = h0_s[...].astype(bf16)
    query = dot_nn(h0, w_ref[0][...]) * SCALE
    to_scratch(images(query, w_ref[1].ready()), qk_s)
    rows_of = lambda q: hid_ref[q][...].reshape(SLOTS * SEQ, D)
    logits = against_rows(qk_s, rows_of)
    valid = [
        jnp.broadcast_to(ids_ref[q, sl : sl + 1, :], (PAD_HEADS, SEQ))
        for sl in range(SLOTS)
        for q in range(QUERIES)
    ]
    valid = jnp.concatenate(valid, axis=0) != 0
    logits = jnp.where(valid, logits, -1e30)
    peak = jnp.max(logits, axis=-1, keepdims=True)
    raw = jnp.where(valid, jnp.exp(logits - peak), 0.0)
    soft = raw / jnp.sum(raw, axis=-1, keepdims=True)
    soft_ref.send(soft)
    z = by_head(sum_rows(soft, rows_of), z_s)
    z_ref.send(z.astype(bf16))
    attended = head_sums(z, wv_ref[2].ready())
    keep = [
        jnp.broadcast_to(column(mask_ref[sl : sl + 1, :]), (QUERIES, 128)) for sl in range(SLOTS)
    ]
    keep = jnp.where(jnp.concatenate(keep, axis=0) != 0, 1.0, 0.0).astype(bf16)
    row = jnp.concatenate([h0, attended.astype(bf16), keep], axis=1)
    for i in range(PSG_DEV):
        pay_ref[i] = row


def class_kernel(after_ref, vec_ref, wa_ref, out_ref):
    cls_f = vec_ref[3:4, :]
    cls_8 = jnp.broadcast_to(cls_f, (QUERIES, D)).astype(bf16)
    cls_query = dot_nn(cls_8, wa_ref[0][...])
    kq = two_part(dot_nt, jnp.where(head_mask(), cls_query[0:1], 0.0), wa_ref[1][...])
    out_ref[0] = jnp.broadcast_to(cls_query[0:1], (PAD_HEADS, D))
    out_ref[1] = kq
    cls_logit = jnp.sum(kq * cls_f, axis=-1, keepdims=True) * SCALE
    out_ref[2] = jnp.broadcast_to(cls_logit, (PAD_HEADS, D))


def score_kernel(
    got_ref,
    we_ref,
    vec_ref,
    class_ref,
    wa_ref,
    score_ref,
    own_ref,
    normed_ref,
    rscale_ref,
    zagg_ref,
    soft_ref,
    small_ref,
):
    got = got_ref[...].reshape(GROUP, 2 * D + 128)
    h0 = got[:, :D]
    att = got[:, D : 2 * D]
    keep = got[:, 2 * D :]
    lane_one = jnp.where(iota((16, 128), 1) == 0, 1.0, 0.0).astype(bf16)
    present = dot_nt(lane_one, keep)[0:1]
    shape3 = (HEADS, QUERIES, GROUP)
    valid = ((iota(shape3, 2) & (QUERIES - 1)) == iota(shape3, 1)) & (present[None] > 0.5)
    normed_e, rscale_e = norm_parts(h0.astype(f32) + dot_nn(att, we_ref[3][...]))
    normed_ref.send(normed_e)
    rscale_ref.send(jnp.broadcast_to(rscale_e, (GROUP, 128)))
    passage = (normed_e * vec_ref[0:1, :]).astype(bf16)
    cls_f = vec_ref[3:4, :]
    logit = two_part(dot_nt, class_ref[1], passage)[:HEADS] * SCALE
    cls_logit = class_ref[2][:HEADS, 0:1]
    logit3 = jnp.where(valid, logit[:, None, :], -1e30)
    cls_logit = cls_logit[:, None, :]
    peak = jnp.maximum(jnp.max(logit3, axis=-1, keepdims=True), cls_logit)
    raw = jnp.where(valid, jnp.exp(logit3 - peak), 0.0)
    cls_raw = jnp.exp(cls_logit - peak)
    total = jnp.sum(raw, axis=-1, keepdims=True) + cls_raw
    soft = (raw / total).reshape(HEADS * QUERIES, GROUP)
    cls_prob = (cls_raw / total).reshape(HEADS * QUERIES, 1)
    soft_ref[0] = soft
    soft_ref[1] = jnp.broadcast_to(cls_prob, (HEADS * QUERIES, GROUP))
    soft_ref.send()
    zagg = two_part(dot_nn, soft, passage) + cls_prob * cls_f
    zagg_ref.send(zagg)
    pooled = head_sums(zagg, wa_ref[2].ready())
    small_ref[2] = pooled
    pooled_b = jnp.concatenate([pooled, jnp.zeros_like(pooled)], axis=0).astype(bf16)
    normed_a, rscale_a = norm_parts(cls_f + dot_nn(pooled_b, wa_ref[3][...])[:QUERIES])
    small_ref[0] = normed_a
    small_ref[1] = jnp.broadcast_to(rscale_a, (QUERIES, D))
    small_ref.send()
    score = jnp.sum(normed_a * vec_ref[1:2, :] * vec_ref[2:3, :], axis=-1, keepdims=True)
    score = jnp.broadcast_to(score + vec_ref[4:5, 0:1], (QUERIES, 128))
    own_ref.send(score)
    diagonal = iota((QUERIES, 128), 0) == iota((QUERIES, 128), 1)
    row = jnp.sum(jnp.where(diagonal, score, 0.0), axis=0, keepdims=True)
    for j in range(DOC_DEV):
        score_ref[j] = row


def backward_kernel(
    z_ref,
    vec_ref,
    small_ref,
    wa_ref,
    zagg_ref,
    normed_ref,
    soft_ref,
    class_ref,
    rscale_ref,
    we_ref,
    hid_ref,
    soft_e_ref,
    wk_ref,
    pay_ref,
    gatt_ref,
    gmix_ref,
    gpv_ref,
    glogit_ref,
    back_ref,
    wv_s,
    u_s,
):
    half = ROWS // 2

    def pay(at, rows):
        low, high = pack_columns(rows.astype(bf16))
        for i in range(PSG_DEV):
            pay_ref[i, at : at + ROWS, :] = low[i * ROWS : (i + 1) * ROWS]
            pay_ref[i, at + ROWS : at + ROWS + half, :] = high[i * half : (i + 1) * half]

    z_ref.ready()
    for fetched in (zagg_ref, normed_ref, soft_ref, class_ref, rscale_ref):
        fetched.begin()
    we_ref[3].begin()
    we_ref[2].begin()
    pay(0, z_ref[...])
    me = lax.axis_index("psg")
    head = jnp.broadcast_to(vec_ref[2:3, :], (QUERIES, D))
    gmix_a = norm_back(head, vec_ref[1:2, :], small_ref[0], small_ref[1][:, 0:1])
    back_ref[1] = gmix_a
    gmix_a16 = jnp.concatenate([gmix_a, jnp.zeros_like(gmix_a)], axis=0).astype(bf16)
    wa_ref[2].ready()
    for q in range(QUERIES):
        hid_ref[q].begin()
    soft_e_ref.begin()
    wk_ref[1].begin()
    gpool = dot_nt(gmix_a16, wa_ref[3][...])[:QUERIES]
    back_ref[0] = gpool
    back_ref.send()
    gpv = images(gpool, wa_ref[2].ready())
    gpv_ref.send(gpv)
    base = jnp.sum(gpv * zagg_ref[...], axis=-1, keepdims=True)
    normed_e = normed_ref[...]
    gain_e = vec_ref[0:1, :]
    passage = (normed_e * gain_e).astype(bf16)
    along = two_part(dot_nt, gpv, passage)
    soft = soft_ref[0]
    glogit = soft * (along - base) * SCALE
    glogit_ref[0] = glogit
    glogit_ref[1] = jnp.broadcast_to(base, (HEADS * QUERIES, GROUP))
    glogit_ref.send()
    kq_wide = jnp.broadcast_to(class_ref[1][:HEADS, None, :], (HEADS, QUERIES, D))
    kq_wide = kq_wide.reshape(HEADS * QUERIES, D)
    left = jnp.concatenate([glogit, soft], axis=0).astype(bf16)
    right = jnp.concatenate([kq_wide, gpv], axis=0).astype(bf16)
    gpass = dot_tn(left, right)
    gmix_e = norm_back(gpass, gain_e, normed_e, rscale_ref[:, 0:1])
    gmix_ref.send(gmix_e)
    gatt_ref.send(dot_nt(gmix_e.astype(bf16), we_ref[3][...]))
    mine = gatt_ref[pl.ds(pl.multiple_of(me * LOCAL, LOCAL), LOCAL), :]
    to_scratch(images(mine, we_ref[2].ready()), wv_s)
    rows_of = lambda q: hid_ref[q][...].reshape(SLOTS * SEQ, D)
    along_e = against_rows(wv_s, rows_of)
    soft_e = soft_e_ref[...]
    base_e = jnp.sum(soft_e * along_e, axis=-1, keepdims=True)
    u = by_head(sum_rows(soft_e * (along_e - base_e) * SCALE, rows_of), u_s)
    gquery = head_sums(u, wk_ref[1].ready()).astype(bf16)
    for i in range(PSG_DEV):
        for c in range(D // 128):
            pay_ref[i, 288 + 16 * c : 304 + 16 * c, :] = gquery[:, c * 128 : (c + 1) * 128]
    pay(144, u)


EARLY = 64
LATE = 56


def early_kernel(
    all_ref,
    own_ref,
    labels_ref,
    gatt_ref,
    gmix_ref,
    got_ref,
    zagg_ref,
    back_ref,
    small_ref,
    vec_ref,
    soft_ref,
    gpv_ref,
    glogit_ref,
    normed_ref,
    we_ref,
    wa_ref,
    pay_0,
    pay_1,
    pay_2,
    pay_3,
    loss_ref,
    g_ref,
    right_ref,
    left_ref,
    score_ref,
    out_s,
):
    diagonal = iota((QUERIES, 128), 0) == iota((QUERIES, 128), 1)
    row = jnp.sum(jnp.where(diagonal, own_ref[...], 0.0), axis=0, keepdims=True)
    score_ref[...] = row[:, :QUERIES]
    me = lax.axis_index("psg")
    doc = lax.axis_index("doc")
    everything = all_ref[...]
    labels = labels_ref[...]
    lane_labels = jnp.concatenate([labels, jnp.full((1, 120), -1, jnp.int32)], axis=1)
    peak = jnp.max(everything, axis=0)
    total = jnp.sum(jnp.exp(everything - peak[None]), axis=0)
    hits = iota((DOC_DEV, 1, 128), 0) == lane_labels[None]
    label_score = jnp.sum(jnp.where(hits, everything, 0.0), axis=0)
    losses = jnp.log(total) + peak - label_score
    losses = jnp.where(iota((1, 128), 1) < QUERIES, losses, 0.0)
    loss_ref[...] = jnp.sum(losses, axis=1, keepdims=True) / QUERIES
    own_hit = jnp.where(column(labels) == doc, 1.0, 0.0)
    g8 = (jnp.exp(own_ref[:, 0:1] - column(peak)) / column(total) - own_hit) / QUERIES
    g8 = jnp.broadcast_to(g8, (QUERIES, D))
    g16 = jnp.concatenate([g8, g8], axis=0)
    g_ref[...] = g16
    g_group = jnp.concatenate([g16] * PSG_DEV, axis=0)
    g_heads = jnp.concatenate([g8] * HEADS, axis=0)
    got = got_ref[...].reshape(GROUP, 2 * D + 128)
    pick = pick_rows(me * ROWS)
    left_ref[...] = dot_nt(pick, got[:, :D]).astype(bf16)
    right_ref[1] = (gatt_ref[...] * g_group).astype(bf16)
    att_t = dot_nt(pick, got[:, D : 2 * D]).astype(bf16)
    put(out_s, 0, dot_nn(att_t, (gmix_ref[...] * g_group).astype(bf16)), EARLY)
    zagg_t = dot_nt(pick, zagg_ref[...].astype(bf16)).astype(bf16)
    shape3 = (HEADS, 1, D)
    own_head = iota(shape3, 0) == (iota(shape3, 2) >> 6)
    gpool = jnp.where(own_head, (back_ref[0] * g8)[None], 0.0).reshape(HEADS * QUERIES, D)
    put(out_s, 18, dot_nn(zagg_t, gpool.astype(bf16)), EARLY)
    blank = jnp.zeros((120, D), f32)
    pooled = jnp.concatenate([small_ref[2], blank], axis=0).astype(bf16)
    pooled_t = dot_nt(pick, pooled).astype(bf16)
    gmix_a = jnp.concatenate([back_ref[1] * g8, blank], axis=0).astype(bf16)
    put(out_s, 36, dot_nn(pooled_t, gmix_a), EARLY)
    cls_f = vec_ref[3:4, :]
    along = jnp.sum(gpv_ref[...] * cls_f, axis=-1, keepdims=True)
    cls_glogit = soft_ref[1][:, 0:1] * (along - glogit_ref[1][:, 0:1]) * SCALE
    passage = (normed_ref[...] * vec_ref[0:1, :]).astype(bf16)
    m = two_part(dot_nn, glogit_ref[0], passage) + cls_glogit * cls_f
    m_sum = jnp.sum((m * g_heads).reshape(HEADS, QUERIES, D), axis=1)
    m_sum = jnp.concatenate([m_sum, jnp.zeros((PAD_HEADS - HEADS, D), f32)], axis=0)
    right_ref[0] = (dot_nn(got[:, :D], we_ref[0][...]) * g_group).astype(bf16)
    qvec = fold(two_part(dot_nn, m_sum, wa_ref[1][...]), head_mask())
    for c in range(D // 128):
        out_s[pl.ds(54 + c, DOC_DEV, stride=EARLY), :] = jnp.broadcast_to(
            qvec[:, c * 128 : (c + 1) * 128], (DOC_DEV, 128)
        )
    m_hi, m_lo = halves(jnp.concatenate([m_sum] * 8, axis=0))
    m_t = dot_nt(pick, m_hi) + dot_nt(pick, m_lo)
    lane_k = iota((DOC_DEV, 128), 1) >> 4
    m_row = jnp.zeros((DOC_DEV, 128), f32)
    for k in range(SHARE):
        m_row = jnp.where(lane_k == k, m_t[k * DOC_DEV : (k + 1) * DOC_DEV], m_row)
    out_s[pl.ds(60, DOC_DEV, stride=EARLY), :] = m_row
    for r in range(61, EARLY):
        out_s[pl.ds(r, DOC_DEV, stride=EARLY), :] = jnp.zeros((DOC_DEV, 128), f32)
    out = out_s[...].astype(bf16).reshape(4, 8, EARLY, 128)
    for n, pay_ref in enumerate((pay_0, pay_1, pay_2, pay_3)):
        pay_ref.send(out[n])


def late_kernel(recv_ref, left_ref, right_ref, g_ref, pay_0, pay_1, pay_2, pay_3, out_s):
    g16 = g_ref[...]
    gq = []
    gk = jnp.zeros((ROWS, D), f32)
    gv = jnp.zeros((ROWS, D), f32)
    for s in range(PSG_DEV):
        at = slice(s * LOCAL, (s + 1) * LOCAL)
        block = recv_ref[s]
        gv = gv + dot_nn(unpack_columns(block[:96], block[96:144]), head_rows(right_ref[1, at, :]))
        gk = gk + dot_nn(
            unpack_columns(block[144:240], block[240:288]), head_rows(right_ref[0, at, :])
        )
        parts = [block[288 + 16 * c : 304 + 16 * c] for c in range(D // 128)]
        gq.append((jnp.concatenate(parts, axis=1).astype(f32) * g16).astype(bf16))
    put(out_s, 0, dot_nn(left_ref[...], jnp.concatenate(gq, axis=0)), LATE)
    put(out_s, 18, gk, LATE)
    put(out_s, 36, gv, LATE)
    for r in range(54, LATE):
        out_s[pl.ds(r, DOC_DEV, stride=LATE), :] = jnp.zeros((DOC_DEV, 128), f32)
    out = out_s[...].astype(bf16).reshape(4, 8, LATE, 128)
    for n, pay_ref in enumerate((pay_0, pay_1, pay_2, pay_3)):
        pay_ref.send(out[n])


def middle_kernel(*refs):
    late = [ref[...].astype(f32) for ref in refs[:4]]
    early = [ref[...].astype(f32) for ref in refs[4:8]]
    late = (late[0] + late[1]) + (late[2] + late[3])
    early = (early[0] + early[1]) + (early[2] + early[3])
    total = jnp.concatenate([early, late], axis=1).astype(bf16)
    refs[8][...] = total


def finish_kernel(class_ref, vec_ref, *refs):
    out_ref = refs[-1]
    first = lax.axis_index("psg") * ROWS + lax.axis_index("doc") * SHARE
    total = refs[0][0].astype(f32)
    for n in range(1, 8):
        total = total + refs[0][n].astype(f32)
    place = [
        (EARLY, 0, 0),
        (EARLY + 18, 0, 1),
        (EARLY + 36, 0, 2),
        (0, 0, 3),
        (18, 1, 2),
        (36, 1, 3),
    ]
    for at, layer, proj in place:
        for r in range(18):
            out_ref[layer, proj : proj + 1, r * 128 : (r + 1) * 128] = total[at + r : at + r + 1, :]
    cls_f = vec_ref[3:4, :]
    m_row = jnp.broadcast_to(total[60:61, :], (16, 128))
    m_row = jnp.where((iota((16, 128), 1) >> 4) == iota((16, 128), 0), m_row, 0.0)
    expand = (iota((128, D), 0) & (PAD_HEADS - 1)) == (iota((128, D), 1) >> 6)
    expand = jnp.where(expand, 1.0, 0.0).astype(bf16)
    keys = two_part(dot_nn, m_row, expand) * class_ref[0, 0:1, :]
    for k in range(SHARE):
        value = jnp.sum(jnp.where(iota((1, D), 1) == first + k, cls_f, 0.0), axis=-1, keepdims=True)
        for c in range(D // 128):
            lanes = slice(k * D + c * 128, k * D + (c + 1) * 128)
            out_ref[1, 0:1, lanes] = value * total[54 + c : 55 + c, :]
            out_ref[1, 1:2, lanes] = keys[k : k + 1, c * 128 : (c + 1) * 128]


WHOLE = pl.BlockSpec(memory_space=pltpu.VMEM)
SCALAR = pl.BlockSpec(memory_space=pltpu.SMEM)
FAR = pl.BlockSpec(memory_space=pl.ANY)


TOP = "top"


class Fetched:
    def __init__(self, src, dst, sem):
        self.copy = pltpu.make_async_copy(src, dst, sem)
        self.dst = dst
        self.started = False
        self.waiting = True

    def begin(self):
        if not self.started:
            self.copy.start()
            self.started = True

    def ready(self):
        self.begin()
        if self.waiting:
            self.copy.wait()
            self.waiting = False
        return self.dst

    def __getitem__(self, index):
        return self.ready()[index]


class Sent:
    def __init__(self, buf, dst, sem):
        self.buf = buf
        self.copy = pltpu.make_async_copy(buf, dst, sem)
        self.going = False

    def __getitem__(self, index):
        return self.buf[index]

    def __setitem__(self, index, value):
        self.buf[index] = value

    def send(self, value=None):
        if value is not None:
            self.buf[...] = value
        self.copy.start()
        self.going = True


def call(kernel, out_shape, scratch, operands, limit=56, first=99):
    single = not isinstance(out_shape, tuple)
    out_shape = (out_shape,) if single else out_shape
    specs, values, plans, buffers = [], [], [], []
    for operand in operands:
        parts = None
        spec = FAR
        if isinstance(operand, tuple):
            if isinstance(operand[0], pl.BlockSpec):
                spec, operand = operand
            else:
                operand, parts = operand
        if spec is FAR:
            operand = pltpu.with_memory_space_constraint(operand, pltpu.HBM)
            plans.append((len(values), parts))
            size = operand.shape if parts is None else (len(parts),) + operand.shape[1:]
            if parts is TOP:
                size = operand.shape[:2] + (16,) + operand.shape[3:]
            buffers.append(pltpu.VMEM(size, operand.dtype))
        specs.append(spec)
        values.append(operand)
    n_sems = sum(1 if parts in (None, TOP) else len(parts) for _, parts in plans)
    n_in, n_buf, n_out = len(values), len(buffers), len(out_shape)

    def body(*refs):
        ins = list(refs[:n_in])
        outs = refs[n_in : n_in + n_out]
        own = refs[n_in + n_out : -1 - n_buf - n_out]
        bufs = refs[-1 - n_buf - n_out : -1 - n_out]
        out_bufs = refs[-1 - n_out : -1]
        sems = refs[-1]
        started = []
        for (at, parts), buf in zip(plans, bufs):
            if parts is None or parts is TOP:
                ref = ins[at] if parts is None else ins[at].at[:, :, pl.ds(0, 16), :]
                ins[at] = Fetched(ref, buf, sems.at[len(started)])
                started.append(ins[at])
            else:
                ref, ins[at] = ins[at], {}
                for n, part in enumerate(parts):
                    ins[at][part] = Fetched(ref.at[part], buf.at[n], sems.at[len(started)])
                    started.append(ins[at][part])
        for fetched in started[:first]:
            fetched.begin()
        sent = [Sent(*both, sems.at[n_sems + n]) for n, both in enumerate(zip(out_bufs, outs))]
        kernel(*ins, *sent, *own)
        for out in sent:
            if not out.going:
                out.send()
        for fetched in started:
            fetched.ready()
        for out in sent:
            out.copy.wait()

    outs = pl.pallas_call(
        body,
        out_shape=tuple(pltpu.HBM(leaf.shape, leaf.dtype) for leaf in out_shape),
        in_specs=specs,
        out_specs=tuple(FAR for leaf in out_shape),
        scratch_shapes=list(scratch)
        + buffers
        + [pltpu.VMEM(leaf.shape, leaf.dtype) for leaf in out_shape]
        + [pltpu.SemaphoreType.DMA((n_sems + n_out,))],
        compiler_params=pltpu.CompilerParams(vmem_limit_bytes=limit * 1024 * 1024),
        name=kernel.__name__,
    )(*values)
    return outs[0] if single else outs


def hops(blocks, order, step):
    def hop(n):
        return lax.ppermute(blocks[n], "doc", [(j, j ^ (n * step)) for j in range(DOC_DEV)])

    return [hop(n) for n in order]


def per_device(
    hidden,
    token_ids,
    passage_mask,
    labels,
    enc_weights,
    enc_gain,
    agg_weights,
    agg_gain,
    agg_cls,
    head_vector,
    score_bias,
):
    shape = jax.ShapeDtypeStruct
    states = hidden.reshape(QUERIES, SLOTS, SEQ, D)
    vectors = [enc_gain, agg_gain, head_vector, agg_cls.astype(f32), jnp.full((D,), score_bias)]
    vectors = jnp.stack(vectors + [jnp.zeros((D,), f32)] * 3)
    head_scratch = pltpu.VMEM((D // 128, LOCAL * PAD_HEADS, 128), f32)
    pairs = HEADS * QUERIES
    group = shape((GROUP, D), f32)
    pay_1, soft_e, z_rows = call(
        forward_kernel,
        (
            shape((PSG_DEV, LOCAL, 2 * D + 128), bf16),
            shape((LOCAL * PAD_HEADS, SEQ), f32),
            shape((HEADS * LOCAL, D), bf16),
        ),
        [pltpu.VMEM((LOCAL, D), f32), head_scratch, head_scratch],
        (
            (states, TOP),
            (enc_weights, (0, 1)),
            (states, tuple(range(QUERIES))),
            token_ids.reshape(QUERIES, SLOTS, SEQ),
            passage_mask.transpose(1, 2, 0).reshape(SLOTS, QUERIES),
            (enc_weights, (2,)),
        ),
    )
    got = lax.all_to_all(pay_1, "psg", 0, 0, tiled=True)
    class_rows = call(
        class_kernel,
        shape((3, PAD_HEADS, D), f32),
        [],
        (z_rows, vectors, (agg_weights, (0, 1))),
    )
    score, own, normed, rscale, zagg, soft, small = call(
        score_kernel,
        (
            shape((DOC_DEV, 1, 128), f32),
            shape((QUERIES, 128), f32),
            group,
            shape((GROUP, 128), f32),
            shape((pairs, D), f32),
            shape((2, pairs, GROUP), f32),
            shape((3, QUERIES, D), f32),
        ),
        [],
        ((WHOLE, got), (enc_weights, (3,)), vectors, class_rows, (agg_weights, (2, 3))),
        limit=24,
    )
    everything = lax.all_to_all(score, "doc", 0, 0, tiled=True)
    pay_2, gatt, gmix, gpv, glogit, back = call(
        backward_kernel,
        (
            shape((PSG_DEV, 384, 128), bf16),
            group,
            group,
            shape((pairs, D), f32),
            shape((2, pairs, GROUP), f32),
            shape((2, QUERIES, D), f32),
        ),
        [head_scratch, head_scratch],
        (
            z_rows,
            vectors,
            small,
            (agg_weights, (3, 2)),
            zagg,
            normed,
            soft,
            class_rows,
            rscale,
            (enc_weights, (3, 2)),
            (states, tuple(range(QUERIES))),
            soft_e,
            (enc_weights, (1,)),
        ),
    )
    recv = lax.all_to_all(pay_2, "psg", 0, 0, tiled=True)
    e_0, e_1, e_2, e_3, loss, g16, right, left, scores = call(
        early_kernel,
        (
            *[shape((8, EARLY, 128), bf16)] * 4,
            shape((1, 1), f32),
            shape((LOCAL, D), f32),
            shape((2, GROUP, D), bf16),
            shape((ROWS, GROUP), bf16),
            shape((1, QUERIES), f32),
        ),
        [pltpu.VMEM((DOC_DEV * EARLY, 128), f32)],
        (
            everything,
            own,
            labels.reshape(1, QUERIES),
            gatt,
            gmix,
            got,
            zagg,
            back,
            small,
            vectors,
            soft,
            gpv,
            glogit,
            normed,
            (enc_weights, (0,)),
            (agg_weights, (1,)),
        ),
    )
    early = [e_0] + hops((e_0, e_1, e_2, e_3), (2, 1, 3), 1)
    left, early[1] = lax.optimization_barrier((left, early[1]))
    late = call(
        late_kernel,
        (shape((8, LATE, 128), bf16),) * 4,
        [pltpu.VMEM((DOC_DEV * LATE, 128), f32)],
        ((WHOLE, recv), left, right, g16),
        limit=24,
    )
    late = [late[0]] + hops(late, (2, 1, 3), 1)
    shares = call(
        middle_kernel,
        shape((8, EARLY + LATE, 128), bf16),
        [],
        (*late, *early),
    )
    same_y = [[4 * z + y for z in range(8)] for y in range(4)]
    shares = lax.all_to_all(shares, "doc", 0, 0, tiled=True, axis_index_groups=same_y)
    weight_grads = call(
        finish_kernel,
        shape((2, 4, SHARE * D), f32),
        [],
        (class_rows, vectors, (WHOLE, shares)),
        limit=16,
    )
    return (scores.reshape(QUERIES, 1), loss.reshape(()), weight_grads)


def solution(mesh):
    placed = (
        P(None, "doc", "psg", None, None),
        P(None, "doc", "psg", None),
        P(None, "doc", "psg"),
        P(),
        P(),
        P(),
        P(),
        P(),
        P(),
        P(),
        P(),
    )
    return jax.shard_map(
        per_device,
        mesh=mesh,
        in_specs=placed,
        out_specs=(P(None, "doc"), P(), P(None, None, ("psg", "doc"))),
        check_vma=False,
    )
```

```python
import jax
import jax.numpy as jnp
from jax import lax
from jax.experimental import pallas as pl
from jax.experimental.pallas import tpu as pltpu
from jax.sharding import PartitionSpec as P

HEADS = 12
HEAD = 64
D = 768
SEQ = 128
QUERIES = 8
SLOTS = 2
LOCAL = QUERIES * SLOTS
PSG_DEV = 8
DOC_DEV = 32
GROUP = PSG_DEV * LOCAL
ROWS = D // PSG_DEV
SHARE = ROWS // DOC_DEV
PAD_HEADS = 16
SCALE = HEAD ** (-0.5)

f32 = jnp.float32
bf16 = jnp.bfloat16


def dot_nn(a, b):
    return lax.dot_general(a, b, (((1,), (0,)), ((), ())), preferred_element_type=f32)


def dot_nt(a, b):
    return lax.dot_general(a, b, (((1,), (1,)), ((), ())), preferred_element_type=f32)


def dot_tn(a, b):
    return lax.dot_general(a, b, (((0,), (0,)), ((), ())), preferred_element_type=f32)


def halves(x):
    hi = x.astype(bf16)
    lo = (x - hi.astype(f32)).astype(bf16)
    return hi, lo


def two_part(dot, x, w):
    n = x.shape[0]
    both = dot(jnp.concatenate(halves(x), axis=0), w)
    return both[:n] + both[n:]


def iota(shape, dim):
    return lax.broadcasted_iota(jnp.int32, shape, dim)


def head_mask():
    return iota((PAD_HEADS, D), 0) == (iota((PAD_HEADS, D), 1) >> 6)


def spread(rows, mask):
    n = rows.shape[0]
    wide = jnp.where(mask[None], rows[:, None, :], 0.0)
    return wide.reshape(n * PAD_HEADS, D)


def fold(rows, mask):
    n = rows.shape[0] // PAD_HEADS
    wide = jnp.where(mask[None], rows.reshape(n, PAD_HEADS, D), 0.0)
    return jnp.sum(wide, axis=1)


QUAD = 4 * HEAD


def quad_mask():
    return iota((4, 1, QUAD), 0) == (iota((4, 1, QUAD), 2) >> 6)


def images(rows, w):
    n = rows.shape[0]
    parts = []
    for at in range(0, D, QUAD):
        wide = jnp.where(quad_mask(), rows[None, :, at : at + QUAD], 0.0).reshape(4 * n, QUAD)
        parts.append(two_part(dot_nt, wide, w[:, at : at + QUAD]))
    return jnp.concatenate(parts, axis=0)


def head_sums(rows, w):
    n = rows.shape[0] // HEADS
    parts = []
    for g, at in enumerate(range(0, D, QUAD)):
        out = two_part(dot_nn, rows[4 * n * g : 4 * n * (g + 1)], w[:, at : at + QUAD])
        parts.append(jnp.sum(jnp.where(quad_mask(), out.reshape(4, n, QUAD), 0.0), axis=0))
    return jnp.concatenate(parts, axis=1)


def norm_parts(x):
    center = x - jnp.mean(x, axis=-1, keepdims=True)
    rscale = lax.rsqrt(jnp.mean(center * center, axis=-1, keepdims=True) + 1e-05)
    return center * rscale, rscale


def norm_back(grad_out, gain, normed, rscale):
    grad_norm = grad_out * gain
    return rscale * (
        grad_norm
        - jnp.mean(grad_norm, axis=-1, keepdims=True)
        - normed * jnp.mean(grad_norm * normed, axis=-1, keepdims=True)
    )


def pick_rows(first):
    me = lax.axis_index("doc")
    r = iota((ROWS, D), 0)
    place = (((r & 7) << 2) + ((r >> 3) & 3)) ^ (me & 3)
    want = first + SHARE * place + (r >> 5)
    return jnp.where(iota((ROWS, D), 1) == want, 1.0, 0.0).astype(bf16)


def column(row):
    n = row.shape[1]
    wide = jnp.broadcast_to(row, (QUERIES, n))
    hit = iota((QUERIES, n), 0) == iota((QUERIES, n), 1)
    return jnp.sum(jnp.where(hit, wide, jnp.zeros_like(wide)), axis=1, keepdims=True)


def pack_columns(rows):
    half = ROWS // 2
    out = dot_nt(jnp.concatenate([pick_rows(ROWS * i) for i in range(PSG_DEV)], axis=0), rows)
    rest = out[:, 128:]
    high = [
        jnp.concatenate([rest[at : at + half], rest[at + half : at + ROWS]], axis=1)
        for at in range(0, D, ROWS)
    ]
    return out[:, :128].astype(bf16), jnp.concatenate(high, axis=0).astype(bf16)


def unpack_columns(low, high):
    both = jnp.concatenate([high, high], axis=0)
    keep = (iota((ROWS, 128), 0) < ROWS // 2) == (iota((ROWS, 128), 1) < 64)
    both = jnp.where(keep, both, jnp.zeros_like(both))
    return jnp.concatenate([low, both], axis=1)


def head_rows(rows):
    shape = (16, 1, D)
    head = iota(shape, 0)
    head = jnp.where(head < HEADS, head, head - 4)
    keep = head == (iota(shape, 2) >> 6)
    return jnp.where(keep, rows[None], jnp.zeros_like(rows)[None]).reshape(16 * LOCAL, D)


def put(out_s, at, rows, pay):
    for k in range(SHARE):
        for c in range(D // 128):
            out_s[pl.ds(at + k * (D // 128) + c, DOC_DEV, stride=pay), :] = rows[
                k * DOC_DEV : (k + 1) * DOC_DEV, c * 128 : (c + 1) * 128
            ]


def heads_at(p):
    return slice(p * PAD_HEADS, (p + 1) * PAD_HEADS)


def to_scratch(rows, scratch):
    for c in range(D // 128):
        scratch[c, : HEADS * LOCAL, :] = rows[:, c * 128 : (c + 1) * 128]
        scratch[c, HEADS * LOCAL :, :] = jnp.zeros(((PAD_HEADS - HEADS) * LOCAL, 128), f32)


def against_rows(scratch, rows_of):
    parts = [None] * LOCAL
    for q in range(QUERIES):
        rows = rows_of(q)
        for sl in range(SLOTS):
            p = sl * QUERIES + q
            x = [scratch[c, pl.ds(p, PAD_HEADS, stride=LOCAL), :] for c in range(D // 128)]
            left = jnp.concatenate(halves(jnp.concatenate(x, axis=1)), axis=0)
            out = dot_nt(left, rows[sl * SEQ : (sl + 1) * SEQ])
            parts[p] = out[:PAD_HEADS] + out[PAD_HEADS:]
    return jnp.concatenate(parts, axis=0)


def sum_rows(x, rows_of):
    hi, lo = halves(x)
    parts = [None] * LOCAL
    blank = jnp.zeros((PAD_HEADS, SEQ), bf16)
    for q in range(QUERIES):
        a, b = heads_at(q), heads_at(QUERIES + q)
        left = [[hi[a], blank], [blank, hi[b]], [lo[a], blank], [blank, lo[b]]]
        left = jnp.concatenate([jnp.concatenate(row, axis=1) for row in left], axis=0)
        out = dot_nn(left, rows_of(q))
        parts[q] = out[0:16] + out[32:48]
        parts[QUERIES + q] = out[16:32] + out[48:64]
    return parts


def by_head(parts, scratch):
    for p, part in enumerate(parts):
        for c in range(D // 128):
            scratch[c, pl.ds(p, PAD_HEADS, stride=LOCAL), :] = part[:, c * 128 : (c + 1) * 128]
    return jnp.concatenate([scratch[c, : HEADS * LOCAL, :] for c in range(D // 128)], axis=1)


def forward_kernel(
    top_ref, w_ref, hid_ref, ids_ref, mask_ref, wv_ref, pay_ref, soft_ref, z_ref, h0_s, qk_s, z_s
):
    for sl in range(SLOTS):
        for q in range(QUERIES):
            p = sl * QUERIES + q
            h0_s[p : p + 1, :] = top_ref[q, sl].astype(f32)[0:1, :]
    h0 = h0_s[...].astype(bf16)
    query = dot_nn(h0, w_ref[0][...]) * SCALE
    to_scratch(images(query, w_ref[1].ready()), qk_s)
    rows_of = lambda q: hid_ref[q][...].reshape(SLOTS * SEQ, D)
    logits = against_rows(qk_s, rows_of)
    valid = [
        jnp.broadcast_to(ids_ref[q, sl : sl + 1, :], (PAD_HEADS, SEQ))
        for sl in range(SLOTS)
        for q in range(QUERIES)
    ]
    valid = jnp.concatenate(valid, axis=0) != 0
    logits = jnp.where(valid, logits, -1e30)
    peak = jnp.max(logits, axis=-1, keepdims=True)
    raw = jnp.where(valid, jnp.exp(logits - peak), 0.0)
    soft = raw / jnp.sum(raw, axis=-1, keepdims=True)
    soft_ref.send(soft)
    z = by_head(sum_rows(soft, rows_of), z_s)
    z_ref.send(z.astype(bf16))
    attended = head_sums(z, wv_ref[2].ready())
    keep = [
        jnp.broadcast_to(column(mask_ref[sl : sl + 1, :]), (QUERIES, 128)) for sl in range(SLOTS)
    ]
    keep = jnp.where(jnp.concatenate(keep, axis=0) != 0, 1.0, 0.0).astype(bf16)
    pay_ref[...] = jnp.concatenate([h0, attended.astype(bf16), keep], axis=1)


def class_kernel(after_ref, vec_ref, wa_ref, out_ref):
    cls_f = vec_ref[3:4, :]
    cls_8 = jnp.broadcast_to(cls_f, (QUERIES, D)).astype(bf16)
    cls_query = dot_nn(cls_8, wa_ref[0][...])
    kq = two_part(dot_nt, jnp.where(head_mask(), cls_query[0:1], 0.0), wa_ref[1][...])
    out_ref[0] = jnp.broadcast_to(cls_query[0:1], (PAD_HEADS, D))
    out_ref[1] = kq
    cls_logit = jnp.sum(kq * cls_f, axis=-1, keepdims=True) * SCALE
    out_ref[2] = jnp.broadcast_to(cls_logit, (PAD_HEADS, D))


def score_kernel(
    we_ref,
    vec_ref,
    class_ref,
    wa_ref,
    *refs,
):
    got_ref, score_ref, own_ref, normed_ref, rscale_ref, zagg_ref, soft_ref, small_ref = refs[8:]
    got = jnp.concatenate([ref[...] for ref in refs[:8]], axis=0)
    got_ref.send(got[:, : 2 * D])
    h0 = got[:, :D]
    att = got[:, D : 2 * D]
    keep = got[:, 2 * D :]
    lane_one = jnp.where(iota((16, 128), 1) == 0, 1.0, 0.0).astype(bf16)
    present = dot_nt(lane_one, keep)[0:1]
    shape3 = (HEADS, QUERIES, GROUP)
    valid = ((iota(shape3, 2) & (QUERIES - 1)) == iota(shape3, 1)) & (present[None] > 0.5)
    normed_e, rscale_e = norm_parts(h0.astype(f32) + dot_nn(att, we_ref[3][...]))
    normed_ref.send(normed_e)
    rscale_ref.send(jnp.broadcast_to(rscale_e, (GROUP, 128)))
    passage = (normed_e * vec_ref[0:1, :]).astype(bf16)
    cls_f = vec_ref[3:4, :]
    logit = two_part(dot_nt, class_ref[1], passage)[:HEADS] * SCALE
    cls_logit = class_ref[2][:HEADS, 0:1]
    logit3 = jnp.where(valid, logit[:, None, :], -1e30)
    cls_logit = cls_logit[:, None, :]
    peak = jnp.maximum(jnp.max(logit3, axis=-1, keepdims=True), cls_logit)
    raw = jnp.where(valid, jnp.exp(logit3 - peak), 0.0)
    cls_raw = jnp.exp(cls_logit - peak)
    total = jnp.sum(raw, axis=-1, keepdims=True) + cls_raw
    soft = (raw / total).reshape(HEADS * QUERIES, GROUP)
    cls_prob = (cls_raw / total).reshape(HEADS * QUERIES, 1)
    soft_ref[0] = soft
    soft_ref[1] = jnp.broadcast_to(cls_prob, (HEADS * QUERIES, GROUP))
    soft_ref.send()
    zagg = two_part(dot_nn, soft, passage) + cls_prob * cls_f
    zagg_ref.send(zagg)
    pooled = head_sums(zagg, wa_ref[2].ready())
    small_ref[2] = pooled
    pooled_b = jnp.concatenate([pooled, jnp.zeros_like(pooled)], axis=0).astype(bf16)
    normed_a, rscale_a = norm_parts(cls_f + dot_nn(pooled_b, wa_ref[3][...])[:QUERIES])
    small_ref[0] = normed_a
    small_ref[1] = jnp.broadcast_to(rscale_a, (QUERIES, D))
    small_ref.send()
    score = jnp.sum(normed_a * vec_ref[1:2, :] * vec_ref[2:3, :], axis=-1, keepdims=True)
    score = jnp.broadcast_to(score + vec_ref[4:5, 0:1], (QUERIES, 128))
    own_ref.send(score)
    diagonal = iota((QUERIES, 128), 0) == iota((QUERIES, 128), 1)
    row = jnp.sum(jnp.where(diagonal, score, 0.0), axis=0, keepdims=True)
    for j in range(DOC_DEV):
        score_ref[j] = row


def backward_kernel(
    z_ref,
    vec_ref,
    small_ref,
    wa_ref,
    zagg_ref,
    normed_ref,
    soft_ref,
    class_ref,
    rscale_ref,
    we_ref,
    hid_ref,
    soft_e_ref,
    wk_ref,
    pay_ref,
    gatt_ref,
    gmix_ref,
    gpv_ref,
    glogit_ref,
    back_ref,
    wv_s,
    u_s,
):
    half = ROWS // 2

    def pay(at, rows):
        low, high = pack_columns(rows.astype(bf16))
        for i in range(PSG_DEV):
            pay_ref[i, at : at + ROWS, :] = low[i * ROWS : (i + 1) * ROWS]
            pay_ref[i, at + ROWS : at + ROWS + half, :] = high[i * half : (i + 1) * half]

    z_ref.ready()
    for fetched in (zagg_ref, normed_ref, soft_ref, class_ref, rscale_ref):
        fetched.begin()
    we_ref[3].begin()
    we_ref[2].begin()
    pay(0, z_ref[...])
    head = jnp.broadcast_to(vec_ref[2:3, :], (QUERIES, D))
    gmix_a = norm_back(head, vec_ref[1:2, :], small_ref[0], small_ref[1][:, 0:1])
    back_ref[1] = gmix_a
    gmix_a16 = jnp.concatenate([gmix_a, jnp.zeros_like(gmix_a)], axis=0).astype(bf16)
    wa_ref[2].ready()
    for q in range(QUERIES):
        hid_ref[q].begin()
    soft_e_ref.begin()
    wk_ref[1].begin()
    gpool = dot_nt(gmix_a16, wa_ref[3][...])[:QUERIES]
    back_ref[0] = gpool
    back_ref.send()
    gpv = images(gpool, wa_ref[2].ready())
    gpv_ref.send(gpv)
    base = jnp.sum(gpv * zagg_ref[...], axis=-1, keepdims=True)
    normed_e = normed_ref[...]
    gain_e = vec_ref[0:1, :]
    passage = (normed_e * gain_e).astype(bf16)
    along = two_part(dot_nt, gpv, passage)
    soft = soft_ref[0]
    glogit = soft * (along - base) * SCALE
    glogit_ref[0] = glogit
    glogit_ref[1] = jnp.broadcast_to(base, (HEADS * QUERIES, GROUP))
    glogit_ref.send()
    kq_wide = jnp.broadcast_to(class_ref[1][:HEADS, None, :], (HEADS, QUERIES, D))
    kq_wide = kq_wide.reshape(HEADS * QUERIES, D)
    left = jnp.concatenate([glogit, soft], axis=0).astype(bf16)
    right = jnp.concatenate([kq_wide, gpv], axis=0).astype(bf16)
    gpass = dot_tn(left, right)
    gmix_e = norm_back(gpass, gain_e, normed_e, rscale_ref[:, 0:1])
    gmix_ref.send(gmix_e)
    gatt_ref.send(dot_nt(gmix_e.astype(bf16), we_ref[3][...]))
    mine = gatt_ref[0:LOCAL, :]
    to_scratch(images(mine, we_ref[2].ready()), wv_s)
    rows_of = lambda q: hid_ref[q][...].reshape(SLOTS * SEQ, D)
    along_e = against_rows(wv_s, rows_of)
    soft_e = soft_e_ref[...]
    base_e = jnp.sum(soft_e * along_e, axis=-1, keepdims=True)
    u = by_head(sum_rows(soft_e * (along_e - base_e) * SCALE, rows_of), u_s)
    gquery = head_sums(u, wk_ref[1].ready()).astype(bf16)
    for i in range(PSG_DEV):
        for c in range(D // 128):
            pay_ref[i, 288 + 16 * c : 304 + 16 * c, :] = gquery[:, c * 128 : (c + 1) * 128]
    pay(144, u)


EARLY = 64
LATE = 56


def early_kernel(
    all_ref,
    own_ref,
    labels_ref,
    gatt_ref,
    gmix_ref,
    got_ref,
    zagg_ref,
    back_ref,
    small_ref,
    vec_ref,
    soft_ref,
    gpv_ref,
    glogit_ref,
    normed_ref,
    we_ref,
    wa_ref,
    pay_0,
    pay_1,
    pay_2,
    pay_3,
    loss_ref,
    g_ref,
    right_ref,
    left_ref,
    score_ref,
    out_s,
):
    diagonal = iota((QUERIES, 128), 0) == iota((QUERIES, 128), 1)
    row = jnp.sum(jnp.where(diagonal, own_ref[...], 0.0), axis=0, keepdims=True)
    score_ref[...] = row[:, :QUERIES]
    me = lax.axis_index("psg")
    doc = lax.axis_index("doc")
    everything = all_ref[...]
    labels = labels_ref[...]
    lane_labels = jnp.concatenate([labels, jnp.full((1, 120), -1, jnp.int32)], axis=1)
    peak = jnp.max(everything, axis=0)
    total = jnp.sum(jnp.exp(everything - peak[None]), axis=0)
    hits = iota((DOC_DEV, 1, 128), 0) == lane_labels[None]
    label_score = jnp.sum(jnp.where(hits, everything, 0.0), axis=0)
    losses = jnp.log(total) + peak - label_score
    losses = jnp.where(iota((1, 128), 1) < QUERIES, losses, 0.0)
    loss_ref[...] = jnp.sum(losses, axis=1, keepdims=True) / QUERIES
    own_hit = jnp.where(column(labels) == doc, 1.0, 0.0)
    g8 = (jnp.exp(own_ref[:, 0:1] - column(peak)) / column(total) - own_hit) / QUERIES
    g8 = jnp.broadcast_to(g8, (QUERIES, D))
    g16 = jnp.concatenate([g8, g8], axis=0)
    g_ref[...] = g16
    g_group = jnp.concatenate([g16] * PSG_DEV, axis=0)
    g_heads = jnp.concatenate([g8] * HEADS, axis=0)
    got = got_ref[...]
    pick = pick_rows(me * ROWS)
    left_ref[...] = dot_nt(pick, got[:, :D]).astype(bf16)
    right_ref[1] = (gatt_ref[...] * g_group).astype(bf16)
    att_t = dot_nt(pick, got[:, D : 2 * D]).astype(bf16)
    put(out_s, 0, dot_nn(att_t, (gmix_ref[...] * g_group).astype(bf16)), EARLY)
    zagg_t = dot_nt(pick, zagg_ref[...].astype(bf16)).astype(bf16)
    shape3 = (HEADS, 1, D)
    own_head = iota(shape3, 0) == (iota(shape3, 2) >> 6)
    gpool = jnp.where(own_head, (back_ref[0] * g8)[None], 0.0).reshape(HEADS * QUERIES, D)
    put(out_s, 18, dot_nn(zagg_t, gpool.astype(bf16)), EARLY)
    blank = jnp.zeros((120, D), f32)
    pooled = jnp.concatenate([small_ref[2], blank], axis=0).astype(bf16)
    pooled_t = dot_nt(pick, pooled).astype(bf16)
    gmix_a = jnp.concatenate([back_ref[1] * g8, blank], axis=0).astype(bf16)
    put(out_s, 36, dot_nn(pooled_t, gmix_a), EARLY)
    cls_f = vec_ref[3:4, :]
    along = jnp.sum(gpv_ref[...] * cls_f, axis=-1, keepdims=True)
    cls_glogit = soft_ref[1][:, 0:1] * (along - glogit_ref[1][:, 0:1]) * SCALE
    passage = (normed_ref[...] * vec_ref[0:1, :]).astype(bf16)
    m = two_part(dot_nn, glogit_ref[0], passage) + cls_glogit * cls_f
    m_sum = jnp.sum((m * g_heads).reshape(HEADS, QUERIES, D), axis=1)
    m_sum = jnp.concatenate([m_sum, jnp.zeros((PAD_HEADS - HEADS, D), f32)], axis=0)
    right_ref[0] = (dot_nn(got[:, :D], we_ref[0][...]) * g_group).astype(bf16)
    qvec = fold(two_part(dot_nn, m_sum, wa_ref[1][...]), head_mask())
    for c in range(D // 128):
        out_s[pl.ds(54 + c, DOC_DEV, stride=EARLY), :] = jnp.broadcast_to(
            qvec[:, c * 128 : (c + 1) * 128], (DOC_DEV, 128)
        )
    m_hi, m_lo = halves(jnp.concatenate([m_sum] * 8, axis=0))
    m_t = dot_nt(pick, m_hi) + dot_nt(pick, m_lo)
    lane_k = iota((DOC_DEV, 128), 1) >> 4
    m_row = jnp.zeros((DOC_DEV, 128), f32)
    for k in range(SHARE):
        m_row = jnp.where(lane_k == k, m_t[k * DOC_DEV : (k + 1) * DOC_DEV], m_row)
    out_s[pl.ds(60, DOC_DEV, stride=EARLY), :] = m_row
    for r in range(61, EARLY):
        out_s[pl.ds(r, DOC_DEV, stride=EARLY), :] = jnp.zeros((DOC_DEV, 128), f32)
    out = out_s[...].astype(bf16).reshape(4, 8, EARLY, 128)
    for n, pay_ref in enumerate((pay_0, pay_1, pay_2, pay_3)):
        pay_ref.send(out[n])


def late_kernel(recv_ref, left_ref, right_ref, g_ref, pay_0, pay_1, pay_2, pay_3, out_s):
    g16 = g_ref[...]
    gq = []
    gk = jnp.zeros((ROWS, D), f32)
    gv = jnp.zeros((ROWS, D), f32)
    for s in range(PSG_DEV):
        at = slice(s * LOCAL, (s + 1) * LOCAL)
        block = recv_ref[lax.axis_index("psg") ^ s]
        gv = gv + dot_nn(unpack_columns(block[:96], block[96:144]), head_rows(right_ref[1, at, :]))
        gk = gk + dot_nn(
            unpack_columns(block[144:240], block[240:288]), head_rows(right_ref[0, at, :])
        )
        parts = [block[288 + 16 * c : 304 + 16 * c] for c in range(D // 128)]
        gq.append((jnp.concatenate(parts, axis=1).astype(f32) * g16).astype(bf16))
    put(out_s, 0, dot_nn(left_ref[...], jnp.concatenate(gq, axis=0)), LATE)
    put(out_s, 18, gk, LATE)
    put(out_s, 36, gv, LATE)
    for r in range(54, LATE):
        out_s[pl.ds(r, DOC_DEV, stride=LATE), :] = jnp.zeros((DOC_DEV, 128), f32)
    out = out_s[...].astype(bf16).reshape(4, 8, LATE, 128)
    for n, pay_ref in enumerate((pay_0, pay_1, pay_2, pay_3)):
        pay_ref.send(out[n])


def middle_kernel(*refs):
    late = [ref[...].astype(f32) for ref in refs[:4]]
    early = [ref[...].astype(f32) for ref in refs[4:8]]
    late = (late[0] + late[1]) + (late[2] + late[3])
    early = (early[0] + early[1]) + (early[2] + early[3])
    total = jnp.concatenate([early, late], axis=1).astype(bf16)
    refs[8][...] = total


def finish_kernel(class_ref, vec_ref, *refs):
    out_ref = refs[-1]
    first = lax.axis_index("psg") * ROWS + lax.axis_index("doc") * SHARE
    total = refs[0][0].astype(f32)
    for n in range(1, 8):
        total = total + refs[0][n].astype(f32)
    place = [
        (EARLY, 0, 0),
        (EARLY + 18, 0, 1),
        (EARLY + 36, 0, 2),
        (0, 0, 3),
        (18, 1, 2),
        (36, 1, 3),
    ]
    for at, layer, proj in place:
        for r in range(18):
            out_ref[layer, proj : proj + 1, r * 128 : (r + 1) * 128] = total[at + r : at + r + 1, :]
    cls_f = vec_ref[3:4, :]
    m_row = jnp.broadcast_to(total[60:61, :], (16, 128))
    m_row = jnp.where((iota((16, 128), 1) >> 4) == iota((16, 128), 0), m_row, 0.0)
    expand = (iota((128, D), 0) & (PAD_HEADS - 1)) == (iota((128, D), 1) >> 6)
    expand = jnp.where(expand, 1.0, 0.0).astype(bf16)
    keys = two_part(dot_nn, m_row, expand) * class_ref[0, 0:1, :]
    for k in range(SHARE):
        value = jnp.sum(jnp.where(iota((1, D), 1) == first + k, cls_f, 0.0), axis=-1, keepdims=True)
        for c in range(D // 128):
            lanes = slice(k * D + c * 128, k * D + (c + 1) * 128)
            out_ref[1, 0:1, lanes] = value * total[54 + c : 55 + c, :]
            out_ref[1, 1:2, lanes] = keys[k : k + 1, c * 128 : (c + 1) * 128]


WHOLE = pl.BlockSpec(memory_space=pltpu.VMEM)
SCALAR = pl.BlockSpec(memory_space=pltpu.SMEM)
FAR = pl.BlockSpec(memory_space=pl.ANY)


TOP = "top"


class Fetched:
    def __init__(self, src, dst, sem):
        self.copy = pltpu.make_async_copy(src, dst, sem)
        self.dst = dst
        self.started = False
        self.waiting = True

    def begin(self):
        if not self.started:
            self.copy.start()
            self.started = True

    def ready(self):
        self.begin()
        if self.waiting:
            self.copy.wait()
            self.waiting = False
        return self.dst

    def __getitem__(self, index):
        return self.ready()[index]


class Sent:
    def __init__(self, buf, dst, sem):
        self.buf = buf
        self.copy = pltpu.make_async_copy(buf, dst, sem)
        self.going = False

    def __getitem__(self, index):
        return self.buf[index]

    def __setitem__(self, index, value):
        self.buf[index] = value

    def send(self, value=None):
        if value is not None:
            self.buf[...] = value
        self.copy.start()
        self.going = True


def call(kernel, out_shape, scratch, operands, limit=56, first=99):
    single = not isinstance(out_shape, tuple)
    out_shape = (out_shape,) if single else out_shape
    specs, values, plans, buffers = [], [], [], []
    for operand in operands:
        parts = None
        spec = FAR
        if isinstance(operand, tuple):
            if isinstance(operand[0], pl.BlockSpec):
                spec, operand = operand
            else:
                operand, parts = operand
        if spec is FAR:
            operand = pltpu.with_memory_space_constraint(operand, pltpu.HBM)
            plans.append((len(values), parts))
            size = operand.shape if parts is None else (len(parts),) + operand.shape[1:]
            if parts is TOP:
                size = operand.shape[:2] + (16,) + operand.shape[3:]
            buffers.append(pltpu.VMEM(size, operand.dtype))
        specs.append(spec)
        values.append(operand)
    n_sems = sum(1 if parts in (None, TOP) else len(parts) for _, parts in plans)
    n_in, n_buf, n_out = len(values), len(buffers), len(out_shape)

    def body(*refs):
        ins = list(refs[:n_in])
        outs = refs[n_in : n_in + n_out]
        own = refs[n_in + n_out : -1 - n_buf - n_out]
        bufs = refs[-1 - n_buf - n_out : -1 - n_out]
        out_bufs = refs[-1 - n_out : -1]
        sems = refs[-1]
        started = []
        for (at, parts), buf in zip(plans, bufs):
            if parts is None or parts is TOP:
                ref = ins[at] if parts is None else ins[at].at[:, :, pl.ds(0, 16), :]
                ins[at] = Fetched(ref, buf, sems.at[len(started)])
                started.append(ins[at])
            else:
                ref, ins[at] = ins[at], {}
                for n, part in enumerate(parts):
                    ins[at][part] = Fetched(ref.at[part], buf.at[n], sems.at[len(started)])
                    started.append(ins[at][part])
        for fetched in started[:first]:
            fetched.begin()
        sent = [Sent(*both, sems.at[n_sems + n]) for n, both in enumerate(zip(out_bufs, outs))]
        kernel(*ins, *sent, *own)
        for out in sent:
            if not out.going:
                out.send()
        for fetched in started:
            fetched.ready()
        for out in sent:
            out.copy.wait()

    outs = pl.pallas_call(
        body,
        out_shape=tuple(pltpu.HBM(leaf.shape, leaf.dtype) for leaf in out_shape),
        in_specs=specs,
        out_specs=tuple(FAR for leaf in out_shape),
        scratch_shapes=list(scratch)
        + buffers
        + [pltpu.VMEM(leaf.shape, leaf.dtype) for leaf in out_shape]
        + [pltpu.SemaphoreType.DMA((n_sems + n_out,))],
        compiler_params=pltpu.CompilerParams(vmem_limit_bytes=limit * 1024 * 1024),
        name=kernel.__name__,
    )(*values)
    return outs[0] if single else outs


def psg_hop(x, flip):
    return lax.ppermute(x, "psg", [(i, i ^ flip) for i in range(PSG_DEV)])


def hops(blocks, order, step):
    def hop(n):
        return lax.ppermute(blocks[n], "doc", [(j, j ^ (n * step)) for j in range(DOC_DEV)])

    return [hop(n) for n in order]


def per_device(
    hidden,
    token_ids,
    passage_mask,
    labels,
    enc_weights,
    enc_gain,
    agg_weights,
    agg_gain,
    agg_cls,
    head_vector,
    score_bias,
):
    shape = jax.ShapeDtypeStruct
    states = hidden.reshape(QUERIES, SLOTS, SEQ, D)
    vectors = [enc_gain, agg_gain, head_vector, agg_cls.astype(f32), jnp.full((D,), score_bias)]
    vectors = jnp.stack(vectors + [jnp.zeros((D,), f32)] * 3)
    head_scratch = pltpu.VMEM((D // 128, LOCAL * PAD_HEADS, 128), f32)
    pairs = HEADS * QUERIES
    group = shape((GROUP, D), f32)
    pay_1, soft_e, z_rows = call(
        forward_kernel,
        (
            shape((LOCAL, 2 * D + 128), bf16),
            shape((LOCAL * PAD_HEADS, SEQ), f32),
            shape((HEADS * LOCAL, D), bf16),
        ),
        [pltpu.VMEM((LOCAL, D), f32), head_scratch, head_scratch],
        (
            (states, TOP),
            (enc_weights, (0, 1)),
            (states, tuple(range(QUERIES))),
            token_ids.reshape(QUERIES, SLOTS, SEQ),
            passage_mask.transpose(1, 2, 0).reshape(SLOTS, QUERIES),
            (enc_weights, (2,)),
        ),
    )
    near = {0: pay_1, **{n: psg_hop(pay_1, n) for n in (4, 6, 2)}}
    class_rows = call(
        class_kernel,
        shape((3, PAD_HEADS, D), f32),
        [],
        (z_rows, vectors, (agg_weights, (0, 1))),
    )
    near[2], class_rows = lax.optimization_barrier((near[2], class_rows))
    blocks = {**near, **{n + 1: psg_hop(near[n], 1) for n in (0, 4, 6, 2)}}
    got, score, own, normed, rscale, zagg, soft, small = call(
        score_kernel,
        (
            shape((GROUP, 2 * D), bf16),
            shape((DOC_DEV, 1, 128), f32),
            shape((QUERIES, 128), f32),
            group,
            shape((GROUP, 128), f32),
            shape((pairs, D), f32),
            shape((2, pairs, GROUP), f32),
            shape((3, QUERIES, D), f32),
        ),
        [],
        ((enc_weights, (3,)), vectors, class_rows, (agg_weights, (2, 3)), *[(WHOLE, blocks[n]) for n in range(8)]),
        limit=24,
    )
    everything = lax.all_to_all(score, "doc", 0, 0, tiled=True)
    pay_2, gatt, gmix, gpv, glogit, back = call(
        backward_kernel,
        (
            shape((PSG_DEV, 384, 128), bf16),
            group,
            group,
            shape((pairs, D), f32),
            shape((2, pairs, GROUP), f32),
            shape((2, QUERIES, D), f32),
        ),
        [head_scratch, head_scratch],
        (
            z_rows,
            vectors,
            small,
            (agg_weights, (3, 2)),
            zagg,
            normed,
            soft,
            class_rows,
            rscale,
            (enc_weights, (3, 2)),
            (states, tuple(range(QUERIES))),
            soft_e,
            (enc_weights, (1,)),
        ),
    )
    recv = lax.all_to_all(pay_2, "psg", 0, 0, tiled=True)
    e_0, e_1, e_2, e_3, loss, g16, right, left, scores = call(
        early_kernel,
        (
            *[shape((8, EARLY, 128), bf16)] * 4,
            shape((1, 1), f32),
            shape((LOCAL, D), f32),
            shape((2, GROUP, D), bf16),
            shape((ROWS, GROUP), bf16),
            shape((1, QUERIES), f32),
        ),
        [pltpu.VMEM((DOC_DEV * EARLY, 128), f32)],
        (
            everything,
            own,
            labels.reshape(1, QUERIES),
            gatt,
            gmix,
            got,
            zagg,
            back,
            small,
            vectors,
            soft,
            gpv,
            glogit,
            normed,
            (enc_weights, (0,)),
            (agg_weights, (1,)),
        ),
    )
    early = [e_0] + hops((e_0, e_1, e_2, e_3), (2, 1, 3), 1)
    left, early[1] = lax.optimization_barrier((left, early[1]))
    late = call(
        late_kernel,
        (shape((8, LATE, 128), bf16),) * 4,
        [pltpu.VMEM((DOC_DEV * LATE, 128), f32)],
        ((WHOLE, recv), left, right, g16),
        limit=24,
    )
    late = [late[0]] + hops(late, (2, 1, 3), 1)
    shares = call(
        middle_kernel,
        shape((8, EARLY + LATE, 128), bf16),
        [],
        (*late, *early),
    )
    same_y = [[4 * z + y for z in range(8)] for y in range(4)]
    shares = lax.all_to_all(shares, "doc", 0, 0, tiled=True, axis_index_groups=same_y)
    weight_grads = call(
        finish_kernel,
        shape((2, 4, SHARE * D), f32),
        [],
        (class_rows, vectors, (WHOLE, shares)),
        limit=16,
    )
    return (scores.reshape(QUERIES, 1), loss.reshape(()), weight_grads)


def solution(mesh):
    placed = (
        P(None, "doc", "psg", None, None),
        P(None, "doc", "psg", None),
        P(None, "doc", "psg"),
        P(),
        P(),
        P(),
        P(),
        P(),
        P(),
        P(),
        P(),
    )
    return jax.shard_map(
        per_device,
        mesh=mesh,
        in_specs=placed,
        out_specs=(P(None, "doc"), P(), P(None, None, ("psg", "doc"))),
        check_vma=False,
    )
```

```python
import jax
import jax.numpy as jnp
from jax import lax
from jax.experimental import pallas as pl
from jax.experimental.pallas import tpu as pltpu
from jax.sharding import PartitionSpec as P

HEADS = 12
HEAD = 64
D = 768
SEQ = 128
QUERIES = 8
SLOTS = 2
LOCAL = QUERIES * SLOTS
PSG_DEV = 8
DOC_DEV = 32
GROUP = PSG_DEV * LOCAL
ROWS = D // PSG_DEV
SHARE = ROWS // DOC_DEV
PAD_HEADS = 16
SCALE = HEAD ** (-0.5)

f32 = jnp.float32
bf16 = jnp.bfloat16


def dot_nn(a, b):
    return lax.dot_general(a, b, (((1,), (0,)), ((), ())), preferred_element_type=f32)


def dot_nt(a, b):
    return lax.dot_general(a, b, (((1,), (1,)), ((), ())), preferred_element_type=f32)


def dot_tn(a, b):
    return lax.dot_general(a, b, (((0,), (0,)), ((), ())), preferred_element_type=f32)


def halves(x):
    hi = x.astype(bf16)
    lo = (x - hi.astype(f32)).astype(bf16)
    return hi, lo


def two_part(dot, x, w):
    n = x.shape[0]
    both = dot(jnp.concatenate(halves(x), axis=0), w)
    return both[:n] + both[n:]


def iota(shape, dim):
    return lax.broadcasted_iota(jnp.int32, shape, dim)


def head_mask():
    return iota((PAD_HEADS, D), 0) == (iota((PAD_HEADS, D), 1) >> 6)


def spread(rows, mask):
    n = rows.shape[0]
    wide = jnp.where(mask[None], rows[:, None, :], 0.0)
    return wide.reshape(n * PAD_HEADS, D)


def fold(rows, mask):
    n = rows.shape[0] // PAD_HEADS
    wide = jnp.where(mask[None], rows.reshape(n, PAD_HEADS, D), 0.0)
    return jnp.sum(wide, axis=1)


QUAD = 4 * HEAD


def quad_mask():
    return iota((4, 1, QUAD), 0) == (iota((4, 1, QUAD), 2) >> 6)


def images(rows, w):
    n = rows.shape[0]
    parts = []
    for at in range(0, D, QUAD):
        wide = jnp.where(quad_mask(), rows[None, :, at : at + QUAD], 0.0).reshape(4 * n, QUAD)
        parts.append(two_part(dot_nt, wide, w[:, at : at + QUAD]))
    return jnp.concatenate(parts, axis=0)


def head_sums(rows, w):
    n = rows.shape[0] // HEADS
    parts = []
    for g, at in enumerate(range(0, D, QUAD)):
        out = two_part(dot_nn, rows[4 * n * g : 4 * n * (g + 1)], w[:, at : at + QUAD])
        parts.append(jnp.sum(jnp.where(quad_mask(), out.reshape(4, n, QUAD), 0.0), axis=0))
    return jnp.concatenate(parts, axis=1)


def norm_parts(x):
    center = x - jnp.mean(x, axis=-1, keepdims=True)
    rscale = lax.rsqrt(jnp.mean(center * center, axis=-1, keepdims=True) + 1e-05)
    return center * rscale, rscale


def norm_back(grad_out, gain, normed, rscale):
    grad_norm = grad_out * gain
    return rscale * (
        grad_norm
        - jnp.mean(grad_norm, axis=-1, keepdims=True)
        - normed * jnp.mean(grad_norm * normed, axis=-1, keepdims=True)
    )


def pick_rows(first):
    me = lax.axis_index("doc")
    r = iota((ROWS, D), 0)
    place = (((r & 7) << 2) + ((r >> 3) & 3)) ^ (me & 3)
    want = first + SHARE * place + (r >> 5)
    return jnp.where(iota((ROWS, D), 1) == want, 1.0, 0.0).astype(bf16)


def column(row):
    n = row.shape[1]
    wide = jnp.broadcast_to(row, (QUERIES, n))
    hit = iota((QUERIES, n), 0) == iota((QUERIES, n), 1)
    return jnp.sum(jnp.where(hit, wide, jnp.zeros_like(wide)), axis=1, keepdims=True)


def pack_columns(rows):
    half = ROWS // 2
    out = dot_nt(jnp.concatenate([pick_rows(ROWS * i) for i in range(PSG_DEV)], axis=0), rows)
    rest = out[:, 128:]
    high = [
        jnp.concatenate([rest[at : at + half], rest[at + half : at + ROWS]], axis=1)
        for at in range(0, D, ROWS)
    ]
    return out[:, :128].astype(bf16), jnp.concatenate(high, axis=0).astype(bf16)


def unpack_columns(low, high):
    both = jnp.concatenate([high, high], axis=0)
    keep = (iota((ROWS, 128), 0) < ROWS // 2) == (iota((ROWS, 128), 1) < 64)
    both = jnp.where(keep, both, jnp.zeros_like(both))
    return jnp.concatenate([low, both], axis=1)


def head_rows(rows):
    shape = (16, 1, D)
    head = iota(shape, 0)
    head = jnp.where(head < HEADS, head, head - 4)
    keep = head == (iota(shape, 2) >> 6)
    return jnp.where(keep, rows[None], jnp.zeros_like(rows)[None]).reshape(16 * LOCAL, D)


def put(out_s, at, rows, pay):
    for k in range(SHARE):
        for c in range(D // 128):
            out_s[pl.ds(at + k * (D // 128) + c, DOC_DEV, stride=pay), :] = rows[
                k * DOC_DEV : (k + 1) * DOC_DEV, c * 128 : (c + 1) * 128
            ]


def heads_at(p):
    return slice(p * PAD_HEADS, (p + 1) * PAD_HEADS)


def to_scratch(rows, scratch):
    for c in range(D // 128):
        scratch[c, : HEADS * LOCAL, :] = rows[:, c * 128 : (c + 1) * 128]
        scratch[c, HEADS * LOCAL :, :] = jnp.zeros(((PAD_HEADS - HEADS) * LOCAL, 128), f32)


def against_rows(scratch, rows_of):
    parts = [None] * LOCAL
    for q in range(QUERIES):
        rows = rows_of(q)
        for sl in range(SLOTS):
            p = sl * QUERIES + q
            x = [scratch[c, pl.ds(p, PAD_HEADS, stride=LOCAL), :] for c in range(D // 128)]
            left = jnp.concatenate(halves(jnp.concatenate(x, axis=1)), axis=0)
            out = dot_nt(left, rows[sl * SEQ : (sl + 1) * SEQ])
            parts[p] = out[:PAD_HEADS] + out[PAD_HEADS:]
    return jnp.concatenate(parts, axis=0)


def sum_rows(x, rows_of):
    hi, lo = halves(x)
    parts = [None] * LOCAL
    blank = jnp.zeros((PAD_HEADS, SEQ), bf16)
    for q in range(QUERIES):
        a, b = heads_at(q), heads_at(QUERIES + q)
        left = [[hi[a], blank], [blank, hi[b]], [lo[a], blank], [blank, lo[b]]]
        left = jnp.concatenate([jnp.concatenate(row, axis=1) for row in left], axis=0)
        out = dot_nn(left, rows_of(q))
        parts[q] = out[0:16] + out[32:48]
        parts[QUERIES + q] = out[16:32] + out[48:64]
    return parts


def by_head(parts, scratch):
    for p, part in enumerate(parts):
        for c in range(D // 128):
            scratch[c, pl.ds(p, PAD_HEADS, stride=LOCAL), :] = part[:, c * 128 : (c + 1) * 128]
    return jnp.concatenate([scratch[c, : HEADS * LOCAL, :] for c in range(D // 128)], axis=1)


def forward_kernel(
    top_ref, w_ref, hid_ref, ids_ref, mask_ref, wv_ref, pay_ref, soft_ref, z_ref, h0_s, qk_s, z_s
):
    for sl in range(SLOTS):
        for q in range(QUERIES):
            p = sl * QUERIES + q
            h0_s[p : p + 1, :] = top_ref[q, sl].astype(f32)[0:1, :]
    h0 = h0_s[...].astype(bf16)
    query = dot_nn(h0, w_ref[0][...]) * SCALE
    to_scratch(images(query, w_ref[1].ready()), qk_s)
    rows_of = lambda q: hid_ref[q][...].reshape(SLOTS * SEQ, D)
    logits = against_rows(qk_s, rows_of)
    valid = [
        jnp.broadcast_to(ids_ref[q, sl : sl + 1, :], (PAD_HEADS, SEQ))
        for sl in range(SLOTS)
        for q in range(QUERIES)
    ]
    valid = jnp.concatenate(valid, axis=0) != 0
    logits = jnp.where(valid, logits, -1e30)
    peak = jnp.max(logits, axis=-1, keepdims=True)
    raw = jnp.where(valid, jnp.exp(logits - peak), 0.0)
    soft = raw / jnp.sum(raw, axis=-1, keepdims=True)
    soft_ref.send(soft)
    z = by_head(sum_rows(soft, rows_of), z_s)
    z_ref.send(z.astype(bf16))
    attended = head_sums(z, wv_ref[2].ready())
    keep = [
        jnp.broadcast_to(column(mask_ref[sl : sl + 1, :]), (QUERIES, 128)) for sl in range(SLOTS)
    ]
    keep = jnp.where(jnp.concatenate(keep, axis=0) != 0, 1.0, 0.0).astype(bf16)
    pay_ref[...] = jnp.concatenate([h0, attended.astype(bf16), keep], axis=1)


def class_kernel(after_ref, vec_ref, wa_ref, out_ref):
    cls_f = vec_ref[3:4, :]
    cls_8 = jnp.broadcast_to(cls_f, (QUERIES, D)).astype(bf16)
    cls_query = dot_nn(cls_8, wa_ref[0][...])
    kq = two_part(dot_nt, jnp.where(head_mask(), cls_query[0:1], 0.0), wa_ref[1][...])
    out_ref[0] = jnp.broadcast_to(cls_query[0:1], (PAD_HEADS, D))
    out_ref[1] = kq
    cls_logit = jnp.sum(kq * cls_f, axis=-1, keepdims=True) * SCALE
    out_ref[2] = jnp.broadcast_to(cls_logit, (PAD_HEADS, D))


def score_kernel(
    we_ref,
    vec_ref,
    class_ref,
    wa_ref,
    *refs,
):
    got_ref, score_ref, own_ref, normed_ref, rscale_ref, zagg_ref, soft_ref, small_ref = refs[8:]
    got = jnp.concatenate([ref[...] for ref in refs[:8]], axis=0)
    got_ref.send(got[:, : 2 * D])
    h0 = got[:, :D]
    att = got[:, D : 2 * D]
    keep = got[:, 2 * D :]
    lane_one = jnp.where(iota((16, 128), 1) == 0, 1.0, 0.0).astype(bf16)
    present = dot_nt(lane_one, keep)[0:1]
    shape3 = (HEADS, QUERIES, GROUP)
    valid = ((iota(shape3, 2) & (QUERIES - 1)) == iota(shape3, 1)) & (present[None] > 0.5)
    normed_e, rscale_e = norm_parts(h0.astype(f32) + dot_nn(att, we_ref[3][...]))
    normed_ref.send(normed_e)
    rscale_ref.send(jnp.broadcast_to(rscale_e, (GROUP, 128)))
    passage = (normed_e * vec_ref[0:1, :]).astype(bf16)
    cls_f = vec_ref[3:4, :]
    logit = two_part(dot_nt, class_ref[1], passage)[:HEADS] * SCALE
    cls_logit = class_ref[2][:HEADS, 0:1]
    logit3 = jnp.where(valid, logit[:, None, :], -1e30)
    cls_logit = cls_logit[:, None, :]
    peak = jnp.maximum(jnp.max(logit3, axis=-1, keepdims=True), cls_logit)
    raw = jnp.where(valid, jnp.exp(logit3 - peak), 0.0)
    cls_raw = jnp.exp(cls_logit - peak)
    total = jnp.sum(raw, axis=-1, keepdims=True) + cls_raw
    soft = (raw / total).reshape(HEADS * QUERIES, GROUP)
    cls_prob = (cls_raw / total).reshape(HEADS * QUERIES, 1)
    soft_ref[0] = soft
    soft_ref[1] = jnp.broadcast_to(cls_prob, (HEADS * QUERIES, GROUP))
    soft_ref.send()
    zagg = two_part(dot_nn, soft, passage) + cls_prob * cls_f
    zagg_ref.send(zagg)
    pooled = head_sums(zagg, wa_ref[2].ready())
    small_ref[2] = pooled
    pooled_b = jnp.concatenate([pooled, jnp.zeros_like(pooled)], axis=0).astype(bf16)
    normed_a, rscale_a = norm_parts(cls_f + dot_nn(pooled_b, wa_ref[3][...])[:QUERIES])
    small_ref[0] = normed_a
    small_ref[1] = jnp.broadcast_to(rscale_a, (QUERIES, D))
    small_ref.send()
    score = jnp.sum(normed_a * vec_ref[1:2, :] * vec_ref[2:3, :], axis=-1, keepdims=True)
    score = jnp.broadcast_to(score + vec_ref[4:5, 0:1], (QUERIES, 128))
    own_ref.send(score)
    diagonal = iota((QUERIES, 128), 0) == iota((QUERIES, 128), 1)
    row = jnp.sum(jnp.where(diagonal, score, 0.0), axis=0, keepdims=True)
    for j in range(DOC_DEV):
        score_ref[j] = row


def backward_kernel(
    z_ref,
    vec_ref,
    small_ref,
    wa_ref,
    zagg_ref,
    normed_ref,
    soft_ref,
    class_ref,
    rscale_ref,
    we_ref,
    hid_ref,
    soft_e_ref,
    wk_ref,
    pay_ref,
    gatt_ref,
    gmix_ref,
    gpv_ref,
    glogit_ref,
    back_ref,
    wv_s,
    u_s,
):
    half = ROWS // 2

    def pay(at, rows):
        low, high = pack_columns(rows.astype(bf16))
        for i in range(PSG_DEV):
            pay_ref[i, at : at + ROWS, :] = low[i * ROWS : (i + 1) * ROWS]
            pay_ref[i, at + ROWS : at + ROWS + half, :] = high[i * half : (i + 1) * half]

    z_ref.ready()
    for fetched in (zagg_ref, normed_ref, soft_ref, class_ref, rscale_ref):
        fetched.begin()
    we_ref[3].begin()
    we_ref[2].begin()
    pay(0, z_ref[...])
    head = jnp.broadcast_to(vec_ref[2:3, :], (QUERIES, D))
    gmix_a = norm_back(head, vec_ref[1:2, :], small_ref[0], small_ref[1][:, 0:1])
    back_ref[1] = gmix_a
    gmix_a16 = jnp.concatenate([gmix_a, jnp.zeros_like(gmix_a)], axis=0).astype(bf16)
    wa_ref[2].ready()
    for q in range(QUERIES):
        hid_ref[q].begin()
    soft_e_ref.begin()
    wk_ref[1].begin()
    gpool = dot_nt(gmix_a16, wa_ref[3][...])[:QUERIES]
    back_ref[0] = gpool
    back_ref.send()
    gpv = images(gpool, wa_ref[2].ready())
    gpv_ref.send(gpv)
    base = jnp.sum(gpv * zagg_ref[...], axis=-1, keepdims=True)
    normed_e = normed_ref[...]
    gain_e = vec_ref[0:1, :]
    passage = (normed_e * gain_e).astype(bf16)
    along = two_part(dot_nt, gpv, passage)
    soft = soft_ref[0]
    glogit = soft * (along - base) * SCALE
    glogit_ref[0] = glogit
    glogit_ref[1] = jnp.broadcast_to(base, (HEADS * QUERIES, GROUP))
    glogit_ref.send()
    kq_wide = jnp.broadcast_to(class_ref[1][:HEADS, None, :], (HEADS, QUERIES, D))
    kq_wide = kq_wide.reshape(HEADS * QUERIES, D)
    left = jnp.concatenate([glogit, soft], axis=0).astype(bf16)
    right = jnp.concatenate([kq_wide, gpv], axis=0).astype(bf16)
    gpass = dot_tn(left, right)
    gmix_e = norm_back(gpass, gain_e, normed_e, rscale_ref[:, 0:1])
    gmix_ref.send(gmix_e)
    gatt_ref.send(dot_nt(gmix_e.astype(bf16), we_ref[3][...]))
    mine = gatt_ref[0:LOCAL, :]
    to_scratch(images(mine, we_ref[2].ready()), wv_s)
    rows_of = lambda q: hid_ref[q][...].reshape(SLOTS * SEQ, D)
    along_e = against_rows(wv_s, rows_of)
    soft_e = soft_e_ref[...]
    base_e = jnp.sum(soft_e * along_e, axis=-1, keepdims=True)
    u = by_head(sum_rows(soft_e * (along_e - base_e) * SCALE, rows_of), u_s)
    gquery = head_sums(u, wk_ref[1].ready()).astype(bf16)
    for i in range(PSG_DEV):
        for c in range(D // 128):
            pay_ref[i, 288 + 16 * c : 304 + 16 * c, :] = gquery[:, c * 128 : (c + 1) * 128]
    pay(144, u)


EARLY = 64
LATE = 56


def early_kernel(
    all_ref,
    own_ref,
    labels_ref,
    gmix_ref,
    got_ref,
    zagg_ref,
    back_ref,
    small_ref,
    vec_ref,
    soft_ref,
    gpv_ref,
    glogit_ref,
    normed_ref,
    wa_ref,
    pay_0,
    pay_1,
    pay_2,
    pay_3,
    loss_ref,
    g_ref,
    score_ref,
    out_s,
):
    diagonal = iota((QUERIES, 128), 0) == iota((QUERIES, 128), 1)
    row = jnp.sum(jnp.where(diagonal, own_ref[...], 0.0), axis=0, keepdims=True)
    score_ref[...] = row[:, :QUERIES]
    me = lax.axis_index("psg")
    doc = lax.axis_index("doc")
    everything = all_ref[...]
    labels = labels_ref[...]
    lane_labels = jnp.concatenate([labels, jnp.full((1, 120), -1, jnp.int32)], axis=1)
    peak = jnp.max(everything, axis=0)
    total = jnp.sum(jnp.exp(everything - peak[None]), axis=0)
    hits = iota((DOC_DEV, 1, 128), 0) == lane_labels[None]
    label_score = jnp.sum(jnp.where(hits, everything, 0.0), axis=0)
    losses = jnp.log(total) + peak - label_score
    losses = jnp.where(iota((1, 128), 1) < QUERIES, losses, 0.0)
    loss_ref[...] = jnp.sum(losses, axis=1, keepdims=True) / QUERIES
    own_hit = jnp.where(column(labels) == doc, 1.0, 0.0)
    g8 = (jnp.exp(own_ref[:, 0:1] - column(peak)) / column(total) - own_hit) / QUERIES
    g8 = jnp.broadcast_to(g8, (QUERIES, D))
    g16 = jnp.concatenate([g8, g8], axis=0)
    g_ref[...] = g16
    g_group = jnp.concatenate([g16] * PSG_DEV, axis=0)
    g_heads = jnp.concatenate([g8] * HEADS, axis=0)
    got = got_ref[...]
    pick = pick_rows(me * ROWS)
    att_t = dot_nt(pick, got[:, D : 2 * D]).astype(bf16)
    put(out_s, 0, dot_nn(att_t, (gmix_ref[...] * g_group).astype(bf16)), EARLY)
    zagg_t = dot_nt(pick, zagg_ref[...].astype(bf16)).astype(bf16)
    shape3 = (HEADS, 1, D)
    own_head = iota(shape3, 0) == (iota(shape3, 2) >> 6)
    gpool = jnp.where(own_head, (back_ref[0] * g8)[None], 0.0).reshape(HEADS * QUERIES, D)
    put(out_s, 18, dot_nn(zagg_t, gpool.astype(bf16)), EARLY)
    blank = jnp.zeros((120, D), f32)
    pooled = jnp.concatenate([small_ref[2], blank], axis=0).astype(bf16)
    pooled_t = dot_nt(pick, pooled).astype(bf16)
    gmix_a = jnp.concatenate([back_ref[1] * g8, blank], axis=0).astype(bf16)
    put(out_s, 36, dot_nn(pooled_t, gmix_a), EARLY)
    cls_f = vec_ref[3:4, :]
    along = jnp.sum(gpv_ref[...] * cls_f, axis=-1, keepdims=True)
    cls_glogit = soft_ref[1][:, 0:1] * (along - glogit_ref[1][:, 0:1]) * SCALE
    passage = (normed_ref[...] * vec_ref[0:1, :]).astype(bf16)
    m = two_part(dot_nn, glogit_ref[0], passage) + cls_glogit * cls_f
    m_sum = jnp.sum((m * g_heads).reshape(HEADS, QUERIES, D), axis=1)
    m_sum = jnp.concatenate([m_sum, jnp.zeros((PAD_HEADS - HEADS, D), f32)], axis=0)
    qvec = fold(two_part(dot_nn, m_sum, wa_ref[1][...]), head_mask())
    for c in range(D // 128):
        out_s[pl.ds(54 + c, DOC_DEV, stride=EARLY), :] = jnp.broadcast_to(
            qvec[:, c * 128 : (c + 1) * 128], (DOC_DEV, 128)
        )
    m_hi, m_lo = halves(jnp.concatenate([m_sum] * 8, axis=0))
    m_t = dot_nt(pick, m_hi) + dot_nt(pick, m_lo)
    lane_k = iota((DOC_DEV, 128), 1) >> 4
    m_row = jnp.zeros((DOC_DEV, 128), f32)
    for k in range(SHARE):
        m_row = jnp.where(lane_k == k, m_t[k * DOC_DEV : (k + 1) * DOC_DEV], m_row)
    out_s[pl.ds(60, DOC_DEV, stride=EARLY), :] = m_row
    for r in range(61, EARLY):
        out_s[pl.ds(r, DOC_DEV, stride=EARLY), :] = jnp.zeros((DOC_DEV, 128), f32)
    out = out_s[...].astype(bf16).reshape(4, 8, EARLY, 128)
    for n, pay_ref in enumerate((pay_0, pay_1, pay_2, pay_3)):
        pay_ref.send(out[n])


def side_kernel(g_ref, got_ref, gatt_ref, we_ref, left_ref, right_ref):
    g_group = jnp.concatenate([g_ref[...]] * PSG_DEV, axis=0)
    h0 = got_ref[:, :D]
    left_ref.send(dot_nt(pick_rows(lax.axis_index("psg") * ROWS), h0).astype(bf16))
    right_ref[1] = (gatt_ref[...] * g_group).astype(bf16)
    right_ref[0] = (dot_nn(h0, we_ref[0][...]) * g_group).astype(bf16)


def late_kernel(recv_ref, left_ref, right_ref, g_ref, pay_0, pay_1, pay_2, pay_3, out_s):
    g16 = g_ref[...]
    gq = []
    gk = jnp.zeros((ROWS, D), f32)
    gv = jnp.zeros((ROWS, D), f32)
    for s in range(PSG_DEV):
        at = slice(s * LOCAL, (s + 1) * LOCAL)
        block = recv_ref[lax.axis_index("psg") ^ s]
        gv = gv + dot_nn(unpack_columns(block[:96], block[96:144]), head_rows(right_ref[1, at, :]))
        gk = gk + dot_nn(
            unpack_columns(block[144:240], block[240:288]), head_rows(right_ref[0, at, :])
        )
        parts = [block[288 + 16 * c : 304 + 16 * c] for c in range(D // 128)]
        gq.append((jnp.concatenate(parts, axis=1).astype(f32) * g16).astype(bf16))
    put(out_s, 0, dot_nn(left_ref[...], jnp.concatenate(gq, axis=0)), LATE)
    put(out_s, 18, gk, LATE)
    put(out_s, 36, gv, LATE)
    for r in range(54, LATE):
        out_s[pl.ds(r, DOC_DEV, stride=LATE), :] = jnp.zeros((DOC_DEV, 128), f32)
    out = out_s[...].astype(bf16).reshape(4, 8, LATE, 128)
    for n, pay_ref in enumerate((pay_0, pay_1, pay_2, pay_3)):
        pay_ref.send(out[n])


def early_sum_kernel(*refs):
    parts = [ref[...].astype(f32) for ref in refs[:4]]
    refs[4][...] = ((parts[0] + parts[1]) + (parts[2] + parts[3])).astype(bf16)


def middle_kernel(early_ref, *refs):
    late = [ref[...].astype(f32) for ref in refs[:4]]
    late = ((late[0] + late[1]) + (late[2] + late[3])).astype(bf16)
    refs[4][...] = jnp.concatenate([early_ref[...], late], axis=1)


def finish_kernel(class_ref, vec_ref, *refs):
    out_ref = refs[-1]
    first = lax.axis_index("psg") * ROWS + lax.axis_index("doc") * SHARE
    total = refs[0][0].astype(f32)
    for n in range(1, 8):
        total = total + refs[0][n].astype(f32)
    place = [
        (EARLY, 0, 0),
        (EARLY + 18, 0, 1),
        (EARLY + 36, 0, 2),
        (0, 0, 3),
        (18, 1, 2),
        (36, 1, 3),
    ]
    for at, layer, proj in place:
        for r in range(18):
            out_ref[layer, proj : proj + 1, r * 128 : (r + 1) * 128] = total[at + r : at + r + 1, :]
    cls_f = vec_ref[3:4, :]
    m_row = jnp.broadcast_to(total[60:61, :], (16, 128))
    m_row = jnp.where((iota((16, 128), 1) >> 4) == iota((16, 128), 0), m_row, 0.0)
    expand = (iota((128, D), 0) & (PAD_HEADS - 1)) == (iota((128, D), 1) >> 6)
    expand = jnp.where(expand, 1.0, 0.0).astype(bf16)
    keys = two_part(dot_nn, m_row, expand) * class_ref[0, 0:1, :]
    for k in range(SHARE):
        value = jnp.sum(jnp.where(iota((1, D), 1) == first + k, cls_f, 0.0), axis=-1, keepdims=True)
        for c in range(D // 128):
            lanes = slice(k * D + c * 128, k * D + (c + 1) * 128)
            out_ref[1, 0:1, lanes] = value * total[54 + c : 55 + c, :]
            out_ref[1, 1:2, lanes] = keys[k : k + 1, c * 128 : (c + 1) * 128]


WHOLE = pl.BlockSpec(memory_space=pltpu.VMEM)
SCALAR = pl.BlockSpec(memory_space=pltpu.SMEM)
FAR = pl.BlockSpec(memory_space=pl.ANY)


TOP = "top"


class Fetched:
    def __init__(self, src, dst, sem):
        self.copy = pltpu.make_async_copy(src, dst, sem)
        self.dst = dst
        self.started = False
        self.waiting = True

    def begin(self):
        if not self.started:
            self.copy.start()
            self.started = True

    def ready(self):
        self.begin()
        if self.waiting:
            self.copy.wait()
            self.waiting = False
        return self.dst

    def __getitem__(self, index):
        return self.ready()[index]


class Sent:
    def __init__(self, buf, dst, sem):
        self.buf = buf
        self.copy = pltpu.make_async_copy(buf, dst, sem)
        self.going = False

    def __getitem__(self, index):
        return self.buf[index]

    def __setitem__(self, index, value):
        self.buf[index] = value

    def send(self, value=None):
        if value is not None:
            self.buf[...] = value
        self.copy.start()
        self.going = True


def call(kernel, out_shape, scratch, operands, limit=56, first=99):
    single = not isinstance(out_shape, tuple)
    out_shape = (out_shape,) if single else out_shape
    specs, values, plans, buffers = [], [], [], []
    for operand in operands:
        parts = None
        spec = FAR
        if isinstance(operand, tuple):
            if isinstance(operand[0], pl.BlockSpec):
                spec, operand = operand
            else:
                operand, parts = operand
        if spec is FAR:
            operand = pltpu.with_memory_space_constraint(operand, pltpu.HBM)
            plans.append((len(values), parts))
            size = operand.shape if parts is None else (len(parts),) + operand.shape[1:]
            if parts is TOP:
                size = operand.shape[:2] + (16,) + operand.shape[3:]
            buffers.append(pltpu.VMEM(size, operand.dtype))
        specs.append(spec)
        values.append(operand)
    n_sems = sum(1 if parts in (None, TOP) else len(parts) for _, parts in plans)
    n_in, n_buf, n_out = len(values), len(buffers), len(out_shape)

    def body(*refs):
        ins = list(refs[:n_in])
        outs = refs[n_in : n_in + n_out]
        own = refs[n_in + n_out : -1 - n_buf - n_out]
        bufs = refs[-1 - n_buf - n_out : -1 - n_out]
        out_bufs = refs[-1 - n_out : -1]
        sems = refs[-1]
        started = []
        for (at, parts), buf in zip(plans, bufs):
            if parts is None or parts is TOP:
                ref = ins[at] if parts is None else ins[at].at[:, :, pl.ds(0, 16), :]
                ins[at] = Fetched(ref, buf, sems.at[len(started)])
                started.append(ins[at])
            else:
                ref, ins[at] = ins[at], {}
                for n, part in enumerate(parts):
                    ins[at][part] = Fetched(ref.at[part], buf.at[n], sems.at[len(started)])
                    started.append(ins[at][part])
        for fetched in started[:first]:
            fetched.begin()
        sent = [Sent(*both, sems.at[n_sems + n]) for n, both in enumerate(zip(out_bufs, outs))]
        kernel(*ins, *sent, *own)
        for out in sent:
            if not out.going:
                out.send()
        for fetched in started:
            fetched.ready()
        for out in sent:
            out.copy.wait()

    outs = pl.pallas_call(
        body,
        out_shape=tuple(pltpu.HBM(leaf.shape, leaf.dtype) for leaf in out_shape),
        in_specs=specs,
        out_specs=tuple(FAR for leaf in out_shape),
        scratch_shapes=list(scratch)
        + buffers
        + [pltpu.VMEM(leaf.shape, leaf.dtype) for leaf in out_shape]
        + [pltpu.SemaphoreType.DMA((n_sems + n_out,))],
        compiler_params=pltpu.CompilerParams(vmem_limit_bytes=limit * 1024 * 1024),
        name=kernel.__name__,
    )(*values)
    return outs[0] if single else outs


def psg_hop(x, flip):
    return lax.ppermute(x, "psg", [(i, i ^ flip) for i in range(PSG_DEV)])


def hops(blocks, order, step):
    def hop(n):
        return lax.ppermute(blocks[n], "doc", [(j, j ^ (n * step)) for j in range(DOC_DEV)])

    return [hop(n) for n in order]


def per_device(
    hidden,
    token_ids,
    passage_mask,
    labels,
    enc_weights,
    enc_gain,
    agg_weights,
    agg_gain,
    agg_cls,
    head_vector,
    score_bias,
):
    shape = jax.ShapeDtypeStruct
    states = hidden.reshape(QUERIES, SLOTS, SEQ, D)
    vectors = [enc_gain, agg_gain, head_vector, agg_cls.astype(f32), jnp.full((D,), score_bias)]
    vectors = jnp.stack(vectors + [jnp.zeros((D,), f32)] * 3)
    head_scratch = pltpu.VMEM((D // 128, LOCAL * PAD_HEADS, 128), f32)
    pairs = HEADS * QUERIES
    group = shape((GROUP, D), f32)
    pay_1, soft_e, z_rows = call(
        forward_kernel,
        (
            shape((LOCAL, 2 * D + 128), bf16),
            shape((LOCAL * PAD_HEADS, SEQ), f32),
            shape((HEADS * LOCAL, D), bf16),
        ),
        [pltpu.VMEM((LOCAL, D), f32), head_scratch, head_scratch],
        (
            (states, TOP),
            (enc_weights, (0, 1)),
            (states, tuple(range(QUERIES))),
            token_ids.reshape(QUERIES, SLOTS, SEQ),
            passage_mask.transpose(1, 2, 0).reshape(SLOTS, QUERIES),
            (enc_weights, (2,)),
        ),
    )
    near = {0: pay_1, **{n: psg_hop(pay_1, n) for n in (4, 6, 2)}}
    class_rows = call(
        class_kernel,
        shape((3, PAD_HEADS, D), f32),
        [],
        (z_rows, vectors, (agg_weights, (0, 1))),
    )
    near[2], class_rows = lax.optimization_barrier((near[2], class_rows))
    blocks = {**near, **{n + 1: psg_hop(near[n], 1) for n in (0, 4, 6, 2)}}
    got, score, own, normed, rscale, zagg, soft, small = call(
        score_kernel,
        (
            shape((GROUP, 2 * D), bf16),
            shape((DOC_DEV, 1, 128), f32),
            shape((QUERIES, 128), f32),
            group,
            shape((GROUP, 128), f32),
            shape((pairs, D), f32),
            shape((2, pairs, GROUP), f32),
            shape((3, QUERIES, D), f32),
        ),
        [],
        ((enc_weights, (3,)), vectors, class_rows, (agg_weights, (2, 3)), *[(WHOLE, blocks[n]) for n in range(8)]),
        limit=24,
    )
    everything = lax.all_to_all(score, "doc", 0, 0, tiled=True)
    pay_2, gatt, gmix, gpv, glogit, back = call(
        backward_kernel,
        (
            shape((PSG_DEV, 384, 128), bf16),
            group,
            group,
            shape((pairs, D), f32),
            shape((2, pairs, GROUP), f32),
            shape((2, QUERIES, D), f32),
        ),
        [head_scratch, head_scratch],
        (
            z_rows,
            vectors,
            small,
            (agg_weights, (3, 2)),
            zagg,
            normed,
            soft,
            class_rows,
            rscale,
            (enc_weights, (3, 2)),
            (states, tuple(range(QUERIES))),
            soft_e,
            (enc_weights, (1,)),
        ),
    )
    recv = lax.all_to_all(pay_2, "psg", 0, 0, tiled=True)
    e_0, e_1, e_2, e_3, loss, g16, scores = call(
        early_kernel,
        (
            *[shape((8, EARLY, 128), bf16)] * 4,
            shape((1, 1), f32),
            shape((LOCAL, D), f32),
            shape((1, QUERIES), f32),
        ),
        [pltpu.VMEM((DOC_DEV * EARLY, 128), f32)],
        (
            everything,
            own,
            labels.reshape(1, QUERIES),
            gmix,
            got,
            zagg,
            back,
            small,
            vectors,
            soft,
            gpv,
            glogit,
            normed,
            (agg_weights, (1,)),
        ),
    )
    left, right = call(
        side_kernel,
        (shape((ROWS, GROUP), bf16), shape((2, GROUP, D), bf16)),
        [],
        (g16, got, gatt, (enc_weights, (0,))),
    )
    early = [e_0] + hops((e_0, e_1, e_2, e_3), (2, 1, 3), 1)
    left, early[1] = lax.optimization_barrier((left, early[1]))
    late = call(
        late_kernel,
        (shape((8, LATE, 128), bf16),) * 4,
        [pltpu.VMEM((DOC_DEV * LATE, 128), f32)],
        ((WHOLE, recv), left, right, g16),
        limit=24,
    )
    g_late, early[0] = lax.optimization_barrier((late[0], early[0]))
    early = call(early_sum_kernel, shape((8, EARLY, 128), bf16), [], tuple(early))
    late = [g_late] + hops(late, (2, 1, 3), 1)
    shares = call(
        middle_kernel,
        shape((8, EARLY + LATE, 128), bf16),
        [],
        (early, *late),
    )
    same_y = [[4 * z + y for z in range(8)] for y in range(4)]
    shares = lax.all_to_all(shares, "doc", 0, 0, tiled=True, axis_index_groups=same_y)
    weight_grads = call(
        finish_kernel,
        shape((2, 4, SHARE * D), f32),
        [],
        (class_rows, vectors, (WHOLE, shares)),
        limit=16,
    )
    return (scores.reshape(QUERIES, 1), loss.reshape(()), weight_grads)


def solution(mesh):
    placed = (
        P(None, "doc", "psg", None, None),
        P(None, "doc", "psg", None),
        P(None, "doc", "psg"),
        P(),
        P(),
        P(),
        P(),
        P(),
        P(),
        P(),
        P(),
    )
    return jax.shard_map(
        per_device,
        mesh=mesh,
        in_specs=placed,
        out_specs=(P(None, "doc"), P(), P(None, None, ("psg", "doc"))),
        check_vma=False,
    )
```
